256 devices in a mesh: wave: 32 (over z, y), lev: 8 (over x, core).
Axes of the slice: x: 4, y: 4, z: 8, core: 2. Of those that a mesh axis runs over, the one named last changes fastest.
Arguments:
- grid_field: bfloat16 [32, 2, 1024, 4224], P('lev', None, 'wave'), may hold values from -6 to 6
- legendre: bfloat16 [512, 1025, 1024], P(('wave', 'lev')), may hold values from -0.1875 to 0.1875
- wave_groups: int32 [512], P(('wave', 'lev')), may hold values from 0 to 511, each once
- lat_weights: float32 [1024], replicated, may hold values from 0.5 to 2
- cycle_points: int32 [2, 1024], replicated, may hold values from 16 to 4116, as said below
- diffusion: float32 [32], replicated, may hold values from 0.5 to 8
Outputs:
- spectrum: float32 [512, 32, 2, 1025], P(('wave', 'lev'))
- grid_out: bfloat16 [32, 2, 1024, 4224], P('lev', None, 'wave')
The draws below stay inside these ranges and needn't reach their ends.
Inputs may be any that keep to these rules, and one draw needn't show every extreme that they name: `wave_groups`: a permutation. cycle_points[h, j] = 16 + 4 j + 4 r with r one of 0, 1, 2; r is 0 on the polar cycles and 2 on the cycles beside the equator.
All inputs are finite; a program needn't handle non-finite values.
Results may differ from the reference program's by a relative error of at most 0.0075.
Values may be sent and summed in bfloat16 or wider, within the bound.
A program may use at most 128 MiB of HBM per device.

```python
import math
import jax
import jax.numpy as jnp
from jax import lax

NLH = 1024
FLD = 32
GROUPS = 512
MW = 1024
K = 1025
NLON = 4224


def draw_cycle_points(key, part):
    key = jax.random.fold_in(key, 7)
    jitter = jax.random.randint(key, (2, NLH), 0, 3)
    cycle_index = jnp.arange(NLH, dtype=jnp.int32)[None, :]
    jitter = jnp.where(cycle_index == 0, 0, jnp.where(cycle_index == NLH - 1, 2, jitter))
    return (16 + 4 * cycle_index + 4 * jitter).astype(jnp.int32)


def shard_levels(stream_key, dims, shards, low, high):
    def one(dim, blocks):
        draws = jax.random.uniform(jax.random.fold_in(jax.random.fold_in(stream_key, 6), dim), (blocks,), jnp.float32, low / len(shards), high / len(shards))
        return jnp.repeat(jnp.exp(draws), dims[dim] // blocks).reshape((-1,) + (1,) * (len(dims) - dim - 1))

    level = one(*shards[0])
    for cut in shards[1:]:
        level = level * one(*cut)
    return level


def noise(stream_key, extent, width, bound, cuts=(), held_as=jnp.bfloat16):
    gain = shard_levels(stream_key, extent, cuts, -0.22, 0.18) if cuts else 1.0
    values = jax.random.normal(stream_key, extent, jnp.float32) * width * gain
    return jnp.minimum(jnp.maximum(values, -bound), bound).astype(held_as)


def setup_inputs(seed: int = 0) -> dict:
    splits = jax.random.split(jax.random.key(seed), 7)
    return {
        "grid_field": noise(splits[0], (FLD, 2, NLH, NLON), 1.0, 6.0, ((0, 8), (2, 32))),
        "legendre": noise(splits[1], (GROUPS, K, NLH), NLH ** -0.5, 0.1875, ((0, 256),)),
        "wave_groups": jax.random.permutation(splits[2], GROUPS).astype(jnp.int32),
        "lat_weights": jnp.clip(jnp.exp(jax.random.uniform(splits[3], (NLH,), jnp.float32, math.log(0.5), math.log(2.0))), 0.5, 2.0),
        "cycle_points": draw_cycle_points(jax.random.fold_in(splits[6], 71), 0),
        "diffusion": jnp.clip(jnp.exp(jax.random.uniform(splits[5], (FLD,), jnp.float32, math.log(0.5), math.log(8.0))), 0.5, 8.0),
    }


def column_waves(wave_groups, total_waves):
    paired = jnp.stack([wave_groups, total_waves - 1 - wave_groups], axis=1).astype(jnp.int32)
    return jnp.repeat(paired.reshape(-1), 2)

def fourier_basis(col_waves, longitudes):
    points = jnp.arange(longitudes, dtype=jnp.int32)
    phase_index = points[:, None] * col_waves[None, :] % longitudes
    angles = phase_index.astype(jnp.float32) * (2.0 * math.pi / longitudes)
    imaginary = jnp.arange(col_waves.shape[0], dtype=jnp.int32) % 2 == 1
    values = jnp.where(imaginary[None, :], -jnp.sin(angles), jnp.cos(angles))
    return (values * (1.0 / math.sqrt(longitudes))).astype(jnp.bfloat16)

def row_layout(wave_ids, total_waves, row_count):
    row_index = jnp.arange(row_count, dtype=jnp.int32)[None, :]
    starts = wave_ids.astype(jnp.int32)[:, None]
    first_member = row_index < total_waves - starts
    parity_second = (row_index - total_waves + starts) % 2
    parity_first = jnp.broadcast_to(row_index % 2, parity_second.shape)
    member = jnp.stack([first_member, jnp.logical_not(first_member)], axis=1)
    parity = jnp.stack([parity_first, parity_second], axis=1)
    selector = jnp.stack([member & (parity == 0), member & (parity == 1)], axis=2)
    degree = jnp.where(first_member, starts + row_index, row_index - 1)
    return (selector, degree)

def damping(degree, diffusion, total_waves):
    level = degree.astype(jnp.float32)
    scaled = level * (level + 1.0) / (total_waves * (total_waves - 1.0))
    return 1.0 / (1.0 + diffusion[None, :, None] * (scaled * scaled)[:, None, :])

def spectral_step(halves, legendre, wave_ids, diffusion, cycle_points, total_waves):
    selector, degree = row_layout(wave_ids, total_waves, legendre.shape[1])
    products = jnp.einsum('gkj,fsjgbr->gfbrsk', legendre.astype(jnp.float32), halves.astype(jnp.float32))
    weights = selector.astype(jnp.float32)[:, None, :, None, :, :]
    spectrum = lax.optimization_barrier(jnp.sum(products * weights, axis=(2, 4)))
    damped = (spectrum * damping(degree, diffusion, total_waves)[:, :, None, :]).astype(jnp.bfloat16)
    spread = weights * damped.astype(jnp.float32)[:, :, None, :, None, :]
    mode_sums = jnp.einsum('gfbrsk,gkj->fsjgbr', spread, legendre.astype(jnp.float32))
    hemispheres = jnp.stack([mode_sums[:, 0] + mode_sums[:, 1], mode_sums[:, 0] - mode_sums[:, 1]], axis=1)
    pair_waves = jnp.stack([wave_ids, total_waves - 1 - wave_ids], axis=1)
    resolved = 2 * pair_waves[None, None, :, :] < cycle_points[:, :, None, None]
    returned = jnp.where(resolved[None, :, :, :, :, None], hemispheres, 0.0).astype(jnp.bfloat16)
    return (spectrum, returned)

def reference(grid_field, legendre, wave_groups, lat_weights, cycle_points, diffusion):
    col_waves = column_waves(wave_groups, MW)
    basis_table = fourier_basis(col_waves, NLON).astype(jnp.float32)
    resolved = 2 * col_waves[None, None, :] < cycle_points[:, :, None]

    def direct_one(one_field):
        fourier = jnp.dot(one_field.astype(jnp.float32).reshape(2 * NLH, NLON), basis_table)
        fourier = jnp.where(resolved, fourier.reshape(2, NLH, 4 * GROUPS), 0.0)
        halves = jnp.stack([fourier[0] + fourier[1], fourier[0] - fourier[1]])
        return (halves * lat_weights[None, :, None]).astype(jnp.bfloat16)
    halves = lax.map(direct_one, grid_field)
    per_slot = jnp.moveaxis(halves.reshape(FLD, 2, NLH, GROUPS, 1, 2, 2), 3, 0)

    def slot_one(slot_items):
        table_slot, wave_slot, half_slot = slot_items
        return spectral_step(half_slot, table_slot[None], wave_slot[None], diffusion, cycle_points, MW)
    spectra, returned = lax.map(slot_one, (legendre, wave_groups, per_slot))
    spectrum = spectra.reshape(GROUPS, FLD, 2, K)
    returned = jnp.moveaxis(returned, 0, 3).reshape(FLD, 2, NLH, 4 * GROUPS)
    doubled = jnp.where(col_waves == 0, 1.0, 2.0).astype(jnp.float32)

    def inverse_one(one_field):
        scaled = one_field.astype(jnp.float32) * doubled[None, None, :]
        values = jnp.dot(scaled.reshape(2 * NLH, 4 * GROUPS), basis_table.T)
        return values.reshape(2, NLH, NLON).astype(jnp.bfloat16)
    grid_out = lax.map(inverse_one, returned)
    return (spectrum, grid_out)
```

```python
import math

import jax
import jax.numpy as jnp
import ml_dtypes
import numpy as np
from jax import lax
from jax.experimental import pallas as pl
from jax.experimental.pallas import tpu as pltpu
from jax.sharding import PartitionSpec as P

WAVES = 1024
PAIRS = 512
NLON = 4224
HALF = NLON // 2
WIDE = 2176
ROWS = 1025
ROWP = 1152
NWAVE = 32
NLEV = 8
MESH = pl.DeviceIdType.MESH
F32 = jnp.float32
BF16 = jnp.bfloat16
NT = (((1,), (1,)), ((), ()))
NN = (((1,), (0,)), ((), ()))


def basis_tables():
    pairs = np.arange(PAIRS, dtype=np.int64)
    points = np.arange(HALF, dtype=np.int64)
    tables = np.zeros((2, 2, PAIRS, WIDE), np.float32)
    for p, waves in enumerate((2 * pairs, WAVES - 1 - 2 * pairs)):
        angles = (waves[:, None] * points[None, :] % NLON) * (2.0 * math.pi / NLON)
        tables[p, 0, :, :HALF] = np.cos(angles) / math.sqrt(NLON)
        tables[p, 1, :, :HALF] = -np.sin(angles) / math.sqrt(NLON)
    return tables.reshape(2, 2 * PAIRS, WIDE).astype(ml_dtypes.bfloat16)


def select8(index, values):
    result = jnp.int32(values[0])
    for k in range(1, len(values)):
        result = jnp.where(index == k, values[k], result)
    return result


Z_ORDER = (0, 1, 7, 2, 6, 3, 5, 4)
Y_ORDER = (0, 1, 3, 2)


def lev_offset(index):
    return select8(index % 4, Y_ORDER), index // 4


def lev_at(l, index):
    dx, dc = lev_offset(index)
    return (l // 2 + dx) % 4 * 2 + (l % 2 + dc) % 2


def lev_from(l, index):
    dx, dc = lev_offset(index)
    return (l // 2 + 4 - dx) % 4 * 2 + (l % 2 + dc) % 2


def wave_at(w, index):
    dz = select8(index % 8, Z_ORDER)
    dy = select8(index // 8, Y_ORDER)
    return (w // 4 + dz) % 8 * 4 + (w % 4 + dy) % 4


def sub_iota(shape):
    return lax.broadcasted_iota(jnp.int32, shape, len(shape) - 2)


def lane_iota(shape):
    return lax.broadcasted_iota(jnp.int32, shape, len(shape) - 1)


def swap_lane(a0, a1, a2, a3):
    lane = lane_iota(a0.shape)
    low64 = lane < 64
    low32 = lane % 64 < 32

    def roll(x, s):
        return pltpu.roll(x, s, 1)

    lo0 = jnp.where(low64, a0, roll(a2, 64))
    lo1 = jnp.where(low64, a1, roll(a3, 64))
    hi0 = jnp.where(low64, roll(a0, 64), a2)
    hi1 = jnp.where(low64, roll(a1, 64), a3)
    return (
        jnp.where(low32, lo0, roll(lo1, 32)),
        jnp.where(low32, roll(lo0, 96), lo1),
        jnp.where(low32, hi0, roll(hi1, 32)),
        jnp.where(low32, roll(hi0, 96), hi1),
    )


def exchange(
    field_hbm, leg_hbm, table_hbm, ids, weights, points, diffusion,
    spec_hbm, back,
    field, raw, leg, last, table, fold, pairs, send_f, recv_f, oper, damp, dope, spec, send_b,
    recv_b, rows, turned, onehot, column, gat1, gat2, gatv, gats,
    s_table, s_field, s_leg, s_local, s_spec, s_g1s, s_g1r, s_g2s, s_g2r, s_fs, s_fr, s_bs, s_br,
):
    w = lax.axis_index("wave")
    l = lax.axis_index("lev")
    me = w * NLEV + l

    field_copy = pltpu.make_async_copy(field_hbm, field, s_field)
    field_copy.start()
    table_copies = [
        pltpu.make_async_copy(table_hbm.at[p], table.at[p], s_table.at[p]) for p in range(2)
    ]
    table_copies[0].start()
    leg_copy = pltpu.make_async_copy(leg_hbm, raw, s_leg)

    barrier = pltpu.get_barrier_semaphore()

    def greet_lev(i, c):
        pl.semaphore_signal(barrier, inc=1, device_id=(w, (l + i) % NLEV), device_id_type=MESH)
        return c

    def greet_wave(i, c):
        pl.semaphore_signal(barrier, inc=1, device_id=((w + i) % NWAVE, l), device_id_type=MESH)
        return c

    lax.fori_loop(1, NLEV, greet_lev, 0)
    lax.fori_loop(1, NWAVE, greet_wave, 0)

    a0 = ids[0]
    a1 = ids[1]
    t0 = jnp.where(a0 % 2 == 0, a0 // 2, (WAVES - 1 - a0) // 2)
    t1 = jnp.where(a1 % 2 == 0, a1 // 2, (WAVES - 1 - a1) // 2)
    flat = sub_iota((8, 128)) * 128 + lane_iota((8, 128))
    tile = jnp.where(flat == 2 * me, t0, 0) + jnp.where(flat == 2 * me + 1, t1, 0)
    tile = tile + jnp.where(flat == PAIRS + t0, 2 * me, 0)
    tile = tile + jnp.where(flat == PAIRS + t1, 2 * me + 1, 0)
    gat1[l] = tile

    band = pl.multiple_of(w // 4 * 128, 128)
    turn = (4 - w % 4) % 4 * 32
    lane1 = lane_iota((8, 128))

    def spread(row):
        moved = pltpu.roll(jnp.broadcast_to(row, (8, 128)), turn, 1)
        first = jnp.where(lane1 < 32, moved, jnp.zeros_like(moved))
        twice = first + pltpu.roll(first, 32, 1)
        return twice + pltpu.roll(twice, 64, 1)

    band_weights = spread(weights[:, pl.ds(band, 128)])
    band_points = [spread(points[h:h + 1, pl.ds(band, 128)]) for h in range(2)]

    pl.semaphore_wait(barrier, NLEV - 1 + NWAVE - 1)

    def send_g1(i, c):
        pltpu.make_async_remote_copy(
            src_ref=gat1.at[l], dst_ref=gat1.at[l], send_sem=s_g1s, recv_sem=s_g1r,
            device_id=(w, (l + i) % NLEV), device_id_type=MESH,
        ).start()
        return c

    lax.fori_loop(1, NLEV, send_g1, 0)

    field_copy.wait()
    table_copies[1].start()

    def fold_body(i, c):
        f = i // 4
        h = i // 2 % 2
        j = pl.multiple_of(i % 2 * 16, 16)
        first = field[f, h, pl.ds(j, 16), 0:WIDE].astype(F32)
        second = field[f, h, pl.ds(j, 16), NLON - WIDE:NLON].astype(F32)
        second = pltpu.roll(second, HALF, 1)
        row = pl.multiple_of(h * 128 + f * 32 + j, 16)
        fold[0, pl.ds(row, 16), :] = (first + second).astype(BF16)
        fold[1, pl.ds(row, 16), :] = (first - second).astype(BF16)
        return c

    lax.fori_loop(0, 16, fold_body, 0)

    g1 = pltpu.make_async_remote_copy(
        src_ref=gat1.at[pl.ds(0, NLEV - 1)], dst_ref=gat1.at[pl.ds(0, NLEV - 1)], send_sem=s_g1s,
        recv_sem=s_g1r, device_id=(w, l), device_id_type=MESH,
    )
    g1.wait_send()
    g1.wait_recv()
    total = gat1[0]
    for i in range(1, NLEV):
        total = total + gat1[i]
    gat2[w] = total

    def send_g2(i, c):
        pltpu.make_async_remote_copy(
            src_ref=gat2.at[w], dst_ref=gat2.at[w], send_sem=s_g2s, recv_sem=s_g2r,
            device_id=((w + i) % NWAVE, l), device_id_type=MESH,
        ).start()
        return c

    lax.fori_loop(1, NWAVE, send_g2, 0)

    def twice_wave(p, pair):
        return 4 * pair if p == 0 else 2 * (WAVES - 1) - 4 * pair

    def transform(p):
        for part in range(2):
            def body(m, c, part=part):
                first = pl.multiple_of(m * 256, 256)
                start = pl.multiple_of(part * PAIRS + m * 256, 256)
                out = lax.dot_general(
                    table[p, pl.ds(start, 256), :], fold[p], NT, preferred_element_type=F32
                )
                twice = twice_wave(p, first + sub_iota((256, 128)))
                north = jnp.where(twice < band_points[0][0:1, :], out[:, :128], 0.0)
                south = jnp.where(twice < band_points[1][0:1, :], out[:, 128:], 0.0)
                scale = band_weights[0:1, :]
                pairs[pl.ds(first, 256), 2 * p + part, :] = (north + south) * scale
                pairs[pl.ds(first, 256), 4 + 2 * p + part, :] = (north - south) * scale
                return c

            lax.fori_loop(0, 2, body, 0)

    table_copies[0].wait()
    transform(0)
    table_copies[1].wait()
    leg_copy.start()
    transform(1)

    g2 = pltpu.make_async_remote_copy(
        src_ref=gat2.at[pl.ds(0, NWAVE - 1)], dst_ref=gat2.at[pl.ds(0, NWAVE - 1)], send_sem=s_g2s,
        recv_sem=s_g2r, device_id=(w, l), device_id_type=MESH,
    )
    g2.wait_send()
    g2.wait_recv()
    total = gat2[0]
    for i in range(1, NWAVE):
        total = total + gat2[i]
    gatv[...] = jnp.clip(total, 0, PAIRS - 1)
    ids_copy = pltpu.make_async_copy(gatv, gats, s_local)
    ids_copy.start()
    ids_copy.wait()

    def packed(d):
        first = gats[d // 64, 2 * d % 128]
        second = gats[d // 64, 2 * d % 128 + 1]
        return jnp.concatenate([pairs[first], pairs[second]], axis=0).astype(BF16)

    recv_f[me] = packed(me)

    def send_forward(i, c):
        j = 256 - i
        w2 = wave_at(w, j % NWAVE)
        l2 = lev_at(l, j // NWAVE)
        d = w2 * NLEV + l2
        send_f[d] = packed(d)
        pltpu.make_async_remote_copy(
            src_ref=send_f.at[d], dst_ref=recv_f.at[me], send_sem=s_fs, recv_sem=s_fr.at[l],
            device_id=(w2, l2), device_id_type=MESH,
        ).start()
        return c

    lax.fori_loop(1, 256, send_forward, 0)

    leg_copy.wait()

    def relay(i, c):
        k = pl.multiple_of(i * 16, 16)
        for ch in range(8):
            x = raw[pl.ds(k, 16), ch].astype(F32)
            for s in range(2):
                leg[s, pl.ds(k, 16), ch * 128:(ch + 1) * 128] = x[:, s, :].astype(BF16)
        return c

    lax.fori_loop(0, 64, relay, 0)
    for ch in range(8):
        x = raw[1024, ch].astype(F32)
        for s in range(2):
            last[s, :, ch * 128:(ch + 1) * 128] = jnp.broadcast_to(x[s:s + 1], (16, 128)).astype(BF16)

    def chosen(a, base, width):
        sub = sub_iota((8, width))
        k = base + lane_iota((8, width))
        is_a = k < WAVES - a
        parity = jnp.where(is_a, k % 2, (k + a) % 2)
        member = jnp.where(is_a, a % 2, 1 - a % 2)
        sel = (sub // 4 == parity) & (sub // 2 % 2 == member) & (k < ROWS)
        degree = jnp.where(is_a, a + k, k - 1)
        return sel, degree

    for s, a in enumerate((a0, a1)):
        sel, degree = chosen(a, 0, ROWP)
        level = degree.astype(F32)
        scaled = level * (level + 1.0) / (WAVES * (WAVES - 1.0))
        squared = scaled * scaled
        one = jnp.where(sel, 1.0, 0.0)

        def damp_body(f, c, s=s, squared=squared, one=one):
            row = pl.multiple_of(f * 8, 8)
            damp[s, pl.ds(row, 8), :] = one / (1.0 + diffusion[f] * squared)
            return c

        lax.fori_loop(0, 32, damp_body, 0)

    for b in range(4):
        holder = gatv[4 + b:5 + b, :]

        def onehot_body(i, c, b=b, holder=holder):
            start = pl.multiple_of(i * 128, 128)
            hit = start + sub_iota((128, 128)) == holder
            onehot[pl.ds(start, 128), b * 128:(b + 1) * 128] = jnp.where(hit, 1.0, 0.0).astype(BF16)
            return c

        lax.fori_loop(0, 4, onehot_body, 0)
    for h in range(2):
        column[h] = jnp.broadcast_to(band_points[h][0:1, :].astype(F32), (128, 128)).T

    def arrive(i, c):
        src = lev_from(l, 7 - i)

        def landed(count):
            pltpu.make_async_remote_copy(
                src_ref=send_f.at[pl.ds(0, count)], dst_ref=recv_f.at[pl.ds(0, count)],
                send_sem=s_fs, recv_sem=s_fr.at[src], device_id=(w, l), device_id_type=MESH,
            ).wait_recv()

        @pl.when(src == l)
        def _():
            landed(NWAVE - 1)

        @pl.when(src != l)
        def _():
            landed(NWAVE)

        for block in range(8):
            tiles = [recv_f[(4 * block + i) * NLEV + src].astype(F32) for i in range(4)]
            by_field = swap_lane(*tiles)
            for s in range(2):
                for pair in range(2):
                    row = pl.multiple_of(src * 32 + pair * 16, 16)
                    oper[s, pl.ds(row, 16), block * 128:(block + 1) * 128] = jnp.concatenate(
                        [
                            by_field[2 * pair][8 * s:8 * s + 8],
                            by_field[2 * pair + 1][8 * s:8 * s + 8],
                        ],
                        axis=0,
                    ).astype(BF16)
        return c

    lax.fori_loop(0, 8, arrive, 0)

    def pick(s, a, x, start, width):
        sel, _ = chosen(a, start, width)
        lanes = pl.ds(start, width)
        for i in range(16):
            damped = []
            for f in (2 * i, 2 * i + 1):
                y = jnp.where(sel, x[8 * f:8 * f + 8], 0.0)
                y = y + pltpu.roll(y, 4, 0)
                y = y + pltpu.roll(y, 2, 0)
                if width == 128:
                    spec[s, f, :, 1024:ROWS] = y[0:2, 0:1]
                else:
                    spec[s, f, :, lanes] = y[0:2]
                damped.append(y * damp[s, 8 * f:8 * f + 8, lanes])
            dope[s, 16 * i:16 * i + 16, lanes] = jnp.concatenate(damped, axis=0).astype(BF16)

    def product(n, c):
        start = pl.multiple_of(n * 256, 256)
        for s, a in enumerate((a0, a1)):
            x = lax.dot_general(
                oper[s], leg[s, pl.ds(start, 256), :], NT, preferred_element_type=F32
            )
            pick(s, a, x, start, 256)
        return c

    lax.fori_loop(0, 4, product, 0)
    for s, a in enumerate((a0, a1)):
        rhs = jnp.concatenate([last[s]] * 8, axis=0)
        x = lax.dot_general(oper[s], rhs, NT, preferred_element_type=F32)
        pick(s, a, x, 1024, 128)
    spec_copy = pltpu.make_async_copy(spec, spec_hbm, s_spec)
    spec_copy.start()

    def inverse(i, c):
        n = (w // 8 + select8(i, (2, 1, 3, 0))) % 4
        start = pl.multiple_of(n * 256, 256)
        sign = jnp.where(sub_iota((1, 8, 256)) < 4, 1.0, -1.0)
        hemis = []
        for s in range(2):
            x = lax.dot_general(
                dope[s, :, 0:1024], leg[s, 0:1024, pl.ds(start, 256)], NN,
                preferred_element_type=F32,
            )
            edge = dope[s, :, 1024:ROWP].astype(F32)[:, 0:1]
            x = x + edge * last[s, :, pl.ds(start, 256)].astype(F32)[0:1]
            x = x.reshape(32, 8, 256)
            hemis.append(x * sign + pltpu.roll(x, 4, 1))
        for l2 in range(8):
            for half in range(2):
                tiles = []
                for f in range(4):
                    tiles.append(
                        jnp.concatenate(
                            [
                                hemis[s][4 * l2 + f, :, half * 128:(half + 1) * 128]
                                for s in range(2)
                            ],
                            axis=0,
                        )
                    )
                for u, x in enumerate(swap_lane(*tiles)):
                    send_b[(8 * n + 4 * half + u) * NLEV + l2] = x.astype(BF16)

        def send_back(m, c):
            w2 = 8 * n + m % 8
            l2 = lev_at(l, 7 - m // 8)
            d = w2 * NLEV + l2

            @pl.when(d != me)
            def _():
                pltpu.make_async_remote_copy(
                    src_ref=send_b.at[d], dst_ref=recv_b.at[me], send_sem=s_bs,
                    recv_sem=s_br.at[w // 8], device_id=(w2, l2), device_id_type=MESH,
                ).start()

            return c

        lax.fori_loop(0, 64, send_back, 0)
        return c

    lax.fori_loop(0, 4, inverse, 0)
    recv_b[me] = send_b[me]

    def returned(i, c):
        n = (w // 8 + 4 - select8(i, (2, 1, 3, 0))) % 4

        def landed(count):
            pltpu.make_async_remote_copy(
                src_ref=send_b.at[pl.ds(0, count)], dst_ref=recv_b.at[pl.ds(0, count)],
                send_sem=s_bs, recv_sem=s_br.at[n], device_id=(w, l), device_id_type=MESH,
            ).wait_recv()

        @pl.when(i == 3)
        def _():
            landed(63)

        @pl.when(i != 3)
        def _():
            landed(64)

        for d in range(64):
            both = recv_b[64 * n + d].astype(F32)
            rows[2 * d] = both[0:8]
            rows[2 * d + 1] = both[8:16]
        lanes = pl.multiple_of(n * 128, 128)
        for j in range(8):
            turned[j, :, pl.ds(lanes, 128)] = rows[:, j, :].T.astype(BF16)
        return c

    lax.fori_loop(0, 4, returned, 0)

    for h in range(2):
        for p in range(2):
            for r in range(2):
                x = lax.dot_general(
                    turned[4 * h + 2 * p + r], onehot[...], NN, preferred_element_type=F32
                )
                limit = jnp.concatenate([column[h]] * 4, axis=1)
                twice = twice_wave(p, lane_iota((128, PAIRS)))
                x = jnp.where(twice.astype(F32) < limit, x, 0.0)
                x = x * (jnp.where(twice == 0, 1.0, 2.0) if p == 0 else 2.0)
                back[p, h * 128:(h + 1) * 128, r * PAIRS:(r + 1) * PAIRS] = x.astype(BF16)

    spec_copy.wait()
    pltpu.make_async_remote_copy(
        src_ref=send_f.at[pl.ds(0, 255)], dst_ref=recv_f.at[pl.ds(0, 255)], send_sem=s_fs,
        recv_sem=s_g1r, device_id=(w, l), device_id_type=MESH,
    ).wait_send()
    pltpu.make_async_remote_copy(
        src_ref=send_b.at[pl.ds(0, 255)], dst_ref=recv_b.at[pl.ds(0, 255)], send_sem=s_bs,
        recv_sem=s_g1r, device_id=(w, l), device_id_type=MESH,
    ).wait_send()


BLOCKS = [(0, 2048, 128)] + [(1 + n, 256 * n, 256) for n in range(8)]


def synthesis(
    back, table_hbm, spec_in, grid_hbm, spec_out, table, outv, s_table, s_spec, s_out
):
    copies = []
    for i, start, width in BLOCKS:
        copies.append(
            pltpu.make_async_copy(
                table_hbm.at[:, :, pl.ds(start, width)], table.at[:, :, pl.ds(start, width)],
                s_table.at[i],
            )
        )
        copies[-1].start()
    spec_copy = pltpu.make_async_copy(spec_in, spec_out, s_spec)
    spec_copy.start()
    outs = []

    def write(x, start, width):
        for h in range(2):
            for f in range(4):
                row = h * 128 + f * 32
                outv[f, h, :, start:start + width] = x[row:row + 32].astype(BF16)
        outs.append(
            pltpu.make_async_copy(
                outv.at[:, :, :, pl.ds(start, width)], grid_hbm.at[:, :, :, pl.ds(start, width)],
                s_out.at[len(outs)],
            )
        )
        outs[-1].start()

    tail = None
    before = None
    for i, start, width in BLOCKS:
        copies[i].wait()
        x = jnp.dot(back[0], table[0, :, start:start + width], preferred_element_type=F32)
        y = jnp.dot(back[1], table[1, :, start:start + width], preferred_element_type=F32)
        total = x + y
        differ = pltpu.roll(x - y, 64, 1)
        if i == 0:
            tail = differ
            before = total
        else:
            low = lane_iota((256, 128)) < 64
            write(total, start, 256)
            edge = jnp.where(low, before, differ[:, :128])
            write(jnp.concatenate([edge, differ[:, 128:]], axis=1), 2048 + start, 256)
            before = differ[:, :128]
    write(jnp.where(lane_iota((256, 128)) < 64, before, tail), 4096, 128)
    for copy in outs:
        copy.wait()
    spec_copy.wait()


def shards(grid_field, legendre, wave_groups, lat_weights, cycle_points, diffusion):
    dma = pltpu.SemaphoreType.DMA
    vmem = pl.BlockSpec(memory_space=pltpu.VMEM)
    smem = pl.BlockSpec(memory_space=pltpu.SMEM)
    hbm = pl.BlockSpec(memory_space=pl.ANY)
    table = jnp.asarray(basis_tables())
    by_row = legendre.reshape(2, ROWS, 8, 128).transpose(1, 2, 0, 3)
    spectrum_shape = (2, 32, 2, ROWS)
    spectrum, back = pl.pallas_call(
        exchange,
        out_shape=(
            jax.ShapeDtypeStruct(spectrum_shape, F32),
            jax.ShapeDtypeStruct((2, 256, 1024), BF16),
        ),
        in_specs=[hbm, hbm, hbm, smem, vmem, vmem, smem],
        out_specs=(hbm, vmem),
        scratch_shapes=[
            pltpu.VMEM((4, 2, 32, NLON), BF16),
            pltpu.VMEM((ROWS, 8, 2, 128), BF16),
            pltpu.VMEM((2, 1024, 1024), BF16),
            pltpu.VMEM((2, 16, 1024), BF16),
            pltpu.VMEM((2, 1024, WIDE), BF16),
            pltpu.VMEM((2, 256, WIDE), BF16),
            pltpu.VMEM((PAIRS, 8, 128), F32),
            pltpu.VMEM((256, 16, 128), BF16),
            pltpu.VMEM((256, 16, 128), BF16),
            pltpu.VMEM((2, 256, 1024), BF16),
            pltpu.VMEM((2, 256, ROWP), F32),
            pltpu.VMEM((2, 256, ROWP), BF16),
            pltpu.VMEM(spectrum_shape, F32),
            pltpu.VMEM((256, 16, 128), BF16),
            pltpu.VMEM((256, 16, 128), BF16),
            pltpu.VMEM((128, 8, 128), F32),
            pltpu.VMEM((8, 128, PAIRS), BF16),
            pltpu.VMEM((PAIRS, PAIRS), BF16),
            pltpu.VMEM((2, 128, 128), F32),
            pltpu.VMEM((NLEV, 8, 128), jnp.int32),
            pltpu.VMEM((NWAVE, 8, 128), jnp.int32),
            pltpu.VMEM((8, 128), jnp.int32),
            pltpu.SMEM((8, 128), jnp.int32),
            dma((2,)), dma, dma, dma, dma, dma, dma, dma, dma, dma, dma((NLEV,)), dma, dma((4,)),
        ],
        compiler_params=pltpu.CompilerParams(
            collective_id=0, has_side_effects=True, vmem_limit_bytes=48 << 20
        ),
        name="exchange",
    )(grid_field, by_row, table, wave_groups, lat_weights.reshape(1, -1), cycle_points, diffusion)
    grid_out, spectrum = pl.pallas_call(
        synthesis,
        out_shape=(
            jax.ShapeDtypeStruct((4, 2, 32, NLON), BF16),
            jax.ShapeDtypeStruct(spectrum_shape, F32),
        ),
        in_specs=[vmem, hbm, hbm],
        out_specs=(hbm, hbm),
        scratch_shapes=[
            pltpu.VMEM((2, 1024, WIDE), BF16),
            pltpu.VMEM((4, 2, 32, NLON), BF16),
            dma((9,)), dma, dma((17,)),
        ],
        compiler_params=pltpu.CompilerParams(vmem_limit_bytes=32 << 20),
        name="synthesis",
    )(back, table, spectrum)
    return spectrum, grid_out


def solution(mesh):
    return jax.shard_map(
        shards,
        mesh=mesh,
        in_specs=(
            P("lev", None, "wave", None),
            P(("wave", "lev"), None, None),
            P(("wave", "lev")),
            P(),
            P(),
            P(),
        ),
        out_specs=(P(("wave", "lev"), None, None, None), P("lev", None, "wave", None)),
        check_vma=False,
    )
```

```python
import math

import jax
import jax.numpy as jnp
import ml_dtypes
import numpy as np
from jax import lax
from jax.experimental import pallas as pl
from jax.experimental.pallas import tpu as pltpu
from jax.sharding import PartitionSpec as P

WAVES = 1024
PAIRS = 512
NLON = 4224
HALF = NLON // 2
WIDE = 2176
ROWS = 1025
ROWP = 1152
NWAVE = 32
NLEV = 8
MESH = pl.DeviceIdType.MESH
F32 = jnp.float32
BF16 = jnp.bfloat16
NT = (((1,), (1,)), ((), ()))
NN = (((1,), (0,)), ((), ()))


def basis_tables():
    pairs = np.arange(PAIRS, dtype=np.int64)
    points = np.arange(HALF, dtype=np.int64)
    tables = np.zeros((2, 2, PAIRS, WIDE), np.float32)
    for p, waves in enumerate((2 * pairs, WAVES - 1 - 2 * pairs)):
        angles = (waves[:, None] * points[None, :] % NLON) * (2.0 * math.pi / NLON)
        tables[p, 0, :, :HALF] = np.cos(angles) / math.sqrt(NLON)
        tables[p, 1, :, :HALF] = -np.sin(angles) / math.sqrt(NLON)
    return tables.reshape(2, 2 * PAIRS, WIDE).astype(ml_dtypes.bfloat16)


def select8(index, values):
    result = jnp.int32(values[0])
    for k in range(1, len(values)):
        result = jnp.where(index == k, values[k], result)
    return result


Z_ORDER = (0, 1, 7, 2, 6, 3, 5, 4)
Y_ORDER = (0, 1, 3, 2)


def lev_offset(index):
    return select8(index % 4, Y_ORDER), index // 4


def lev_at(l, index):
    dx, dc = lev_offset(index)
    return (l // 2 + dx) % 4 * 2 + (l % 2 + dc) % 2


def lev_from(l, index):
    dx, dc = lev_offset(index)
    return (l // 2 + 4 - dx) % 4 * 2 + (l % 2 + dc) % 2


def wave_at(w, index):
    dz = select8(index % 8, Z_ORDER)
    dy = select8(index // 8, Y_ORDER)
    return (w // 4 + dz) % 8 * 4 + (w % 4 + dy) % 4


def sub_iota(shape):
    return lax.broadcasted_iota(jnp.int32, shape, len(shape) - 2)


def lane_iota(shape):
    return lax.broadcasted_iota(jnp.int32, shape, len(shape) - 1)


def swap_lane(a0, a1, a2, a3):
    lane = lane_iota(a0.shape)
    low64 = lane < 64
    low32 = lane % 64 < 32

    def roll(x, s):
        return pltpu.roll(x, s, 1)

    lo0 = jnp.where(low64, a0, roll(a2, 64))
    lo1 = jnp.where(low64, a1, roll(a3, 64))
    hi0 = jnp.where(low64, roll(a0, 64), a2)
    hi1 = jnp.where(low64, roll(a1, 64), a3)
    return (
        jnp.where(low32, lo0, roll(lo1, 32)),
        jnp.where(low32, roll(lo0, 96), lo1),
        jnp.where(low32, hi0, roll(hi1, 32)),
        jnp.where(low32, roll(hi0, 96), hi1),
    )


BLOCKS = [(2048, 128)] + [(256 * n, 256) for n in range(8)]


def exchange(
    field_hbm, leg_hbm, table_hbm, ids_hbm, weights_hbm, points_hbm, diffusion_hbm,
    spec, grid,
    field, raw, leg, last, table, fold, pairs, send_f, recv_f, oper, damp, dope, modes, send_b,
    recv_b, rows, turned, onehot, column, back, gat1, gat2, gatv, gats, ids, weights, points,
    diffusion,
    s_table, s_field, s_leg, s_local, s_small, s_g1s, s_g1r, s_g2s, s_g2r, s_fs, s_fr, s_bs, s_br,
):
    w = lax.axis_index("wave")
    l = lax.axis_index("lev")
    me = w * NLEV + l

    small_copies = [
        pltpu.make_async_copy(a, b, s_small.at[i])
        for i, (a, b) in enumerate((
            (ids_hbm, ids), (weights_hbm, weights), (points_hbm, points), (diffusion_hbm, diffusion),
        ))
    ]
    for copy in small_copies:
        copy.start()
    field_copy = pltpu.make_async_copy(field_hbm, field, s_field)
    field_copy.start()
    table_copies = [
        pltpu.make_async_copy(table_hbm.at[p], table.at[p], s_table.at[p]) for p in range(2)
    ]
    table_copies[0].start()
    leg_copy = pltpu.make_async_copy(leg_hbm, raw, s_leg)

    barrier = pltpu.get_barrier_semaphore()

    def greet_lev(i, c):
        pl.semaphore_signal(barrier, inc=1, device_id=(w, (l + i) % NLEV), device_id_type=MESH)
        return c

    def greet_wave(i, c):
        pl.semaphore_signal(barrier, inc=1, device_id=((w + i) % NWAVE, l), device_id_type=MESH)
        return c

    lax.fori_loop(1, NLEV, greet_lev, 0)
    lax.fori_loop(1, NWAVE, greet_wave, 0)

    for copy in small_copies:
        copy.wait()
    a0 = ids[0]
    a1 = ids[1]
    t0 = jnp.where(a0 % 2 == 0, a0 // 2, (WAVES - 1 - a0) // 2)
    t1 = jnp.where(a1 % 2 == 0, a1 // 2, (WAVES - 1 - a1) // 2)
    flat = sub_iota((8, 128)) * 128 + lane_iota((8, 128))
    tile = jnp.where(flat == 2 * me, t0, 0) + jnp.where(flat == 2 * me + 1, t1, 0)
    tile = tile + jnp.where(flat == PAIRS + t0, 2 * me, 0)
    tile = tile + jnp.where(flat == PAIRS + t1, 2 * me + 1, 0)
    gat1[l] = tile

    band = pl.multiple_of(w // 4 * 128, 128)
    turn = (4 - w % 4) % 4 * 32
    lane1 = lane_iota((8, 128))

    def spread(row):
        moved = pltpu.roll(jnp.broadcast_to(row, (8, 128)), turn, 1)
        first = jnp.where(lane1 < 32, moved, jnp.zeros_like(moved))
        twice = first + pltpu.roll(first, 32, 1)
        return twice + pltpu.roll(twice, 64, 1)

    band_weights = spread(weights[:, pl.ds(band, 128)])
    band_points = [spread(points[h:h + 1, pl.ds(band, 128)]) for h in range(2)]

    pl.semaphore_wait(barrier, NLEV - 1 + NWAVE - 1)

    def send_g1(i, c):
        pltpu.make_async_remote_copy(
            src_ref=gat1.at[l], dst_ref=gat1.at[l], send_sem=s_g1s, recv_sem=s_g1r,
            device_id=(w, (l + i) % NLEV), device_id_type=MESH,
        ).start()
        return c

    lax.fori_loop(1, NLEV, send_g1, 0)

    field_copy.wait()
    table_copies[1].start()

    def fold_body(i, c):
        f = i // 4
        h = i // 2 % 2
        j = pl.multiple_of(i % 2 * 16, 16)
        first = field[f, h, pl.ds(j, 16), 0:WIDE].astype(F32)
        second = field[f, h, pl.ds(j, 16), NLON - WIDE:NLON].astype(F32)
        second = pltpu.roll(second, HALF, 1)
        row = pl.multiple_of(h * 128 + f * 32 + j, 16)
        fold[0, pl.ds(row, 16), :] = (first + second).astype(BF16)
        fold[1, pl.ds(row, 16), :] = (first - second).astype(BF16)
        return c

    lax.fori_loop(0, 16, fold_body, 0)

    g1 = pltpu.make_async_remote_copy(
        src_ref=gat1.at[pl.ds(0, NLEV - 1)], dst_ref=gat1.at[pl.ds(0, NLEV - 1)], send_sem=s_g1s,
        recv_sem=s_g1r, device_id=(w, l), device_id_type=MESH,
    )
    g1.wait_send()
    g1.wait_recv()
    total = gat1[0]
    for i in range(1, NLEV):
        total = total + gat1[i]
    gat2[w] = total

    def send_g2(i, c):
        pltpu.make_async_remote_copy(
            src_ref=gat2.at[w], dst_ref=gat2.at[w], send_sem=s_g2s, recv_sem=s_g2r,
            device_id=((w + i) % NWAVE, l), device_id_type=MESH,
        ).start()
        return c

    lax.fori_loop(1, NWAVE, send_g2, 0)

    def twice_wave(p, pair):
        return 4 * pair if p == 0 else 2 * (WAVES - 1) - 4 * pair

    def transform(p):
        def body(part, c):
            start = pl.multiple_of(part * PAIRS, PAIRS)
            out = lax.dot_general(
                table[p, pl.ds(start, PAIRS), :], fold[p], NT, preferred_element_type=F32
            )
            twice = twice_wave(p, sub_iota((PAIRS, 128)))
            north = jnp.where(twice < band_points[0][0:1, :], out[:, :128], 0.0)
            south = jnp.where(twice < band_points[1][0:1, :], out[:, 128:], 0.0)
            scale = band_weights[0:1, :]
            pairs[:, 2 * p + part, :] = (north + south) * scale
            pairs[:, 4 + 2 * p + part, :] = (north - south) * scale
            return c

        lax.fori_loop(0, 2, body, 0)

    table_copies[0].wait()
    transform(0)
    table_copies[1].wait()
    leg_copy.start()
    transform(1)

    g2 = pltpu.make_async_remote_copy(
        src_ref=gat2.at[pl.ds(0, NWAVE - 1)], dst_ref=gat2.at[pl.ds(0, NWAVE - 1)], send_sem=s_g2s,
        recv_sem=s_g2r, device_id=(w, l), device_id_type=MESH,
    )
    g2.wait_send()
    g2.wait_recv()
    total = gat2[0]
    for i in range(1, NWAVE):
        total = total + gat2[i]
    gatv[...] = jnp.clip(total, 0, PAIRS - 1)
    ids_copy = pltpu.make_async_copy(gatv, gats, s_local)
    ids_copy.start()
    ids_copy.wait()

    def packed(d):
        first = gats[d // 64, 2 * d % 128]
        second = gats[d // 64, 2 * d % 128 + 1]
        return jnp.concatenate([pairs[first], pairs[second]], axis=0).astype(BF16)

    recv_f[me] = packed(me)

    def send_forward(i, c):
        j = 256 - i
        w2 = wave_at(w, j % NWAVE)
        l2 = lev_at(l, j // NWAVE)
        d = w2 * NLEV + l2
        send_f[d] = packed(d)
        pltpu.make_async_remote_copy(
            src_ref=send_f.at[d], dst_ref=recv_f.at[me], send_sem=s_fs, recv_sem=s_fr.at[l],
            device_id=(w2, l2), device_id_type=MESH,
        ).start()
        return c

    lax.fori_loop(1, 256, send_forward, 0, unroll=5)

    leg_copy.wait()

    def relay(i, c):
        k = pl.multiple_of(i * 16, 16)
        for ch in range(8):
            x = raw[pl.ds(k, 16), ch].astype(F32)
            for s in range(2):
                leg[s, pl.ds(k, 16), ch * 128:(ch + 1) * 128] = x[:, s, :].astype(BF16)
        return c

    lax.fori_loop(0, 64, relay, 0)
    for ch in range(8):
        x = raw[1024, ch].astype(F32)
        for s in range(2):
            last[s, :, ch * 128:(ch + 1) * 128] = jnp.broadcast_to(x[s:s + 1], (16, 128)).astype(BF16)

    def chosen(a, base, width):
        sub = sub_iota((8, width))
        k = base + lane_iota((8, width))
        is_a = k < WAVES - a
        parity = jnp.where(is_a, k % 2, (k + a) % 2)
        member = jnp.where(is_a, a % 2, 1 - a % 2)
        sel = (sub // 4 == parity) & (sub // 2 % 2 == member) & (k < ROWS)
        degree = jnp.where(is_a, a + k, k - 1)
        return sel, degree

    for s, a in enumerate((a0, a1)):
        sel, degree = chosen(a, 0, ROWP)
        level = degree.astype(F32)
        scaled = level * (level + 1.0) / (WAVES * (WAVES - 1.0))
        squared = scaled * scaled
        one = jnp.where(sel, 1.0, 0.0)

        def damp_body(f, c, s=s, squared=squared, one=one):
            row = pl.multiple_of(f * 8, 8)
            damp[s, pl.ds(row, 8), :] = one / (1.0 + diffusion[f] * squared)
            return c

        lax.fori_loop(0, 32, damp_body, 0)

    for q in range(4):
        bases = [2 * lev_from(l, 7 - 2 * q - u) for u in range(2)]

        def onehot_body(b, c, q=q, bases=bases):
            sub = sub_iota((128, 128))
            slot = jnp.where(sub < 64, bases[0], bases[1]) + sub % 64 // 2 * 16 + sub % 2
            for b in range(4):
                hit = slot == gatv[4 + b:5 + b, :]
                onehot[q * 128:(q + 1) * 128, b * 128:(b + 1) * 128] = jnp.where(
                    hit, 1.0, 0.0
                ).astype(BF16)
            return c

        lax.fori_loop(0, 1, onehot_body, 0)
    for h in range(2):
        column[h] = jnp.broadcast_to(band_points[h][0:1, :].astype(F32), (128, 128)).T

    def arrive(i, c):
        src = lev_from(l, 7 - i)

        def landed(count):
            pltpu.make_async_remote_copy(
                src_ref=send_f.at[pl.ds(0, count)], dst_ref=recv_f.at[pl.ds(0, count)],
                send_sem=s_fs, recv_sem=s_fr.at[src], device_id=(w, l), device_id_type=MESH,
            ).wait_recv()

        @pl.when(src == l)
        def _():
            landed(NWAVE - 1)

        @pl.when(src != l)
        def _():
            landed(NWAVE)

        for block in range(8):
            tiles = [recv_f[(4 * block + i) * NLEV + src].astype(F32) for i in range(4)]
            by_field = swap_lane(*tiles)
            for s in range(2):
                for pair in range(2):
                    row = pl.multiple_of(src * 32 + pair * 16, 16)
                    oper[s, pl.ds(row, 16), block * 128:(block + 1) * 128] = jnp.concatenate(
                        [
                            by_field[2 * pair][8 * s:8 * s + 8],
                            by_field[2 * pair + 1][8 * s:8 * s + 8],
                        ],
                        axis=0,
                    ).astype(BF16)
        return c

    lax.fori_loop(0, 8, arrive, 0)

    def pick(s, a, x, start, width):
        sel, _ = chosen(a, start, width)
        lanes = pl.ds(start, width)
        for i in range(16):
            damped = []
            for f in (2 * i, 2 * i + 1):
                y = jnp.where(sel, x[8 * f:8 * f + 8], 0.0)
                y = y + pltpu.roll(y, 4, 0)
                y = y + pltpu.roll(y, 2, 0)
                if width == 128:
                    spec[s, f, :, 1024:ROWS] = y[0:2, 0:1]
                else:
                    spec[s, f, :, lanes] = y[0:2]
                damped.append(y * damp[s, 8 * f:8 * f + 8, lanes])
            dope[s, 16 * i:16 * i + 16, lanes] = jnp.concatenate(damped, axis=0).astype(BF16)

    def product(n, c):
        start = pl.multiple_of(n * 256, 256)
        for s, a in enumerate((a0, a1)):
            x = lax.dot_general(
                oper[s], leg[s, pl.ds(start, 256), :], NT, preferred_element_type=F32
            )
            pick(s, a, x, start, 256)
        return c

    lax.fori_loop(0, 4, product, 0, unroll=4)
    for s, a in enumerate((a0, a1)):
        rhs = jnp.concatenate([last[s]] * 8, axis=0)
        x = lax.dot_general(oper[s], rhs, NT, preferred_element_type=F32)
        pick(s, a, x, 1024, 128)

    def inverse(n, c):
        start = pl.multiple_of(n * 256, 256)
        sign = jnp.where(sub_iota((1, 8, 256)) < 4, 1.0, -1.0)
        for s in range(2):
            x = lax.dot_general(
                dope[s, :, 0:1024], leg[s, 0:1024, pl.ds(start, 256)], NN,
                preferred_element_type=F32,
            )
            edge = dope[s, :, 1024:ROWP].astype(F32)[:, 0:1]
            x = x + edge * last[s, :, pl.ds(start, 256)].astype(F32)[0:1]
            x = x.reshape(32, 8, 256)
            modes[s, :, :, pl.ds(start, 256)] = x * sign + pltpu.roll(x, 4, 1)
        return c

    lax.fori_loop(0, 4, inverse, 0, unroll=4)

    def send_group(i, c):
        l2 = lev_at(l, 7 - i)
        for block in range(8):
            lanes = slice(block * 128, (block + 1) * 128)
            tiles = [
                jnp.concatenate([modes[s, 4 * l2 + f, :, lanes] for s in range(2)], axis=0)
                for f in range(4)
            ]
            for u, x in enumerate(swap_lane(*tiles)):
                send_b[(4 * block + u) * NLEV + l2] = x.astype(BF16)

        def send_back(m, c):
            w2 = wave_at(w, 31 - m)
            d = w2 * NLEV + l2

            @pl.when(d != me)
            def _():
                pltpu.make_async_remote_copy(
                    src_ref=send_b.at[d], dst_ref=recv_b.at[me], send_sem=s_bs,
                    recv_sem=s_br.at[l], device_id=(w2, l2), device_id_type=MESH,
                ).start()

            return c

        lax.fori_loop(0, 32, send_back, 0)
        return c

    lax.fori_loop(0, 8, send_group, 0)
    recv_b[me] = send_b[me]

    def returned(q, c):
        for u in range(2):
            src = lev_from(l, 7 - 2 * q - u)

            def landed(count, src=src):
                pltpu.make_async_remote_copy(
                    src_ref=send_b.at[pl.ds(0, count)], dst_ref=recv_b.at[pl.ds(0, count)],
                    send_sem=s_bs, recv_sem=s_br.at[src], device_id=(w, l), device_id_type=MESH,
                ).wait_recv()

            @pl.when(src == l)
            def _():
                landed(NWAVE - 1)

            @pl.when(src != l)
            def _():
                landed(NWAVE)

            for v in range(NWAVE):
                both = recv_b[v * NLEV + src].astype(F32)
                rows[64 * u + 2 * v] = both[0:8]
                rows[64 * u + 2 * v + 1] = both[8:16]
        lanes = pl.multiple_of(q * 128, 128)
        for j in range(8):
            turned[j, :, pl.ds(lanes, 128)] = rows[:, j, :].T.astype(BF16)
        return c

    lax.fori_loop(0, 4, returned, 0)

    for h in range(2):
        for p in range(2):
            for r in range(2):
                x = lax.dot_general(
                    turned[4 * h + 2 * p + r], onehot[...], NN, preferred_element_type=F32
                )
                limit = jnp.concatenate([column[h]] * 4, axis=1)
                twice = twice_wave(p, lane_iota((128, PAIRS)))
                x = jnp.where(twice.astype(F32) < limit, x, 0.0)
                x = x * (jnp.where(twice == 0, 1.0, 2.0) if p == 0 else 2.0)
                back[p, h * 128:(h + 1) * 128, r * PAIRS:(r + 1) * PAIRS] = x.astype(BF16)

    def write(x, start, width):
        for h in range(2):
            for f in range(4):
                row = h * 128 + f * 32
                grid[f, h, :, start:start + width] = x[row:row + 32].astype(BF16)

    tail = None
    before = None
    for start, width in BLOCKS:
        x = jnp.dot(back[0], table[0, :, start:start + width], preferred_element_type=F32)
        y = jnp.dot(back[1], table[1, :, start:start + width], preferred_element_type=F32)
        total = x + y
        differ = pltpu.roll(x - y, 64, 1)
        if width == 128:
            tail = differ
            before = total
        else:
            low = lane_iota((256, 128)) < 64
            write(total, start, 256)
            edge = jnp.where(low, before, differ[:, :128])
            write(jnp.concatenate([edge, differ[:, 128:]], axis=1), 2048 + start, 256)
            before = differ[:, :128]
    write(jnp.where(lane_iota((256, 128)) < 64, before, tail), 4096, 128)

    pltpu.make_async_remote_copy(
        src_ref=send_f.at[pl.ds(0, 255)], dst_ref=recv_f.at[pl.ds(0, 255)], send_sem=s_fs,
        recv_sem=s_g1r, device_id=(w, l), device_id_type=MESH,
    ).wait_send()
    pltpu.make_async_remote_copy(
        src_ref=send_b.at[pl.ds(0, 255)], dst_ref=recv_b.at[pl.ds(0, 255)], send_sem=s_bs,
        recv_sem=s_g1r, device_id=(w, l), device_id_type=MESH,
    ).wait_send()


def shards(grid_field, legendre, wave_groups, lat_weights, cycle_points, diffusion):
    dma = pltpu.SemaphoreType.DMA
    vmem = pl.BlockSpec(memory_space=pltpu.VMEM)
    hbm = pl.BlockSpec(memory_space=pltpu.HBM)
    table = jnp.asarray(basis_tables())
    by_row = legendre.reshape(2, ROWS, 8, 128).transpose(1, 2, 0, 3)
    return pl.pallas_call(
        exchange,
        out_shape=(
            pltpu.VMEM((2, 32, 2, ROWS), F32),
            pltpu.VMEM((4, 2, 32, NLON), BF16),
        ),
        in_specs=[hbm] * 7,
        out_specs=(vmem, vmem),
        scratch_shapes=[
            pltpu.VMEM((4, 2, 32, NLON), BF16),
            pltpu.VMEM((ROWS, 8, 2, 128), BF16),
            pltpu.VMEM((2, 1024, 1024), BF16),
            pltpu.VMEM((2, 16, 1024), BF16),
            pltpu.VMEM((2, 1024, WIDE), BF16),
            pltpu.VMEM((2, 256, WIDE), BF16),
            pltpu.VMEM((PAIRS, 8, 128), F32),
            pltpu.VMEM((256, 16, 128), BF16),
            pltpu.VMEM((256, 16, 128), BF16),
            pltpu.VMEM((2, 256, 1024), BF16),
            pltpu.VMEM((2, 256, ROWP), F32),
            pltpu.VMEM((2, 256, ROWP), BF16),
            pltpu.VMEM((2, 32, 8, 1024), F32),
            pltpu.VMEM((256, 16, 128), BF16),
            pltpu.VMEM((256, 16, 128), BF16),
            pltpu.VMEM((128, 8, 128), F32),
            pltpu.VMEM((8, 128, PAIRS), BF16),
            pltpu.VMEM((PAIRS, PAIRS), BF16),
            pltpu.VMEM((2, 128, 128), F32),
            pltpu.VMEM((2, 256, 1024), BF16),
            pltpu.VMEM((NLEV, 8, 128), jnp.int32),
            pltpu.VMEM((NWAVE, 8, 128), jnp.int32),
            pltpu.VMEM((8, 128), jnp.int32),
            pltpu.SMEM((8, 128), jnp.int32),
            pltpu.SMEM((2,), jnp.int32),
            pltpu.VMEM((1, 1024), F32),
            pltpu.VMEM((2, 1024), jnp.int32),
            pltpu.SMEM((32,), F32),
            dma((2,)), dma, dma, dma, dma((4,)), dma, dma, dma, dma, dma, dma((NLEV,)), dma,
            dma((NLEV,)),
        ],
        compiler_params=pltpu.CompilerParams(
            collective_id=0, has_side_effects=True, vmem_limit_bytes=56 << 20
        ),
        name="exchange",
    )(grid_field, by_row, table, wave_groups, lat_weights.reshape(1, -1), cycle_points, diffusion)


def solution(mesh):
    return jax.shard_map(
        shards,
        mesh=mesh,
        in_specs=(
            P("lev", None, "wave", None),
            P(("wave", "lev"), None, None),
            P(("wave", "lev")),
            P(),
            P(),
            P(),
        ),
        out_specs=(P(("wave", "lev"), None, None, None), P("lev", None, "wave", None)),
        check_vma=False,
    )
```

```python
import math

import jax
import jax.numpy as jnp
import ml_dtypes
import numpy as np
from jax import lax
from jax.experimental import pallas as pl
from jax.experimental.pallas import tpu as pltpu
from jax.sharding import PartitionSpec as P

WAVES = 1024
PAIRS = 512
NLON = 4224
HALF = NLON // 2
WIDE = 2176
ROWS = 1025
ROWP = 1152
NWAVE = 32
NLEV = 8
MESH = pl.DeviceIdType.MESH
F32 = jnp.float32
BF16 = jnp.bfloat16
NT = (((1,), (1,)), ((), ()))
NN = (((1,), (0,)), ((), ()))


def basis_tables():
    pairs = np.arange(PAIRS, dtype=np.int64)
    points = np.arange(HALF, dtype=np.int64)
    tables = np.zeros((2, 2, PAIRS, WIDE), np.float32)
    for p, waves in enumerate((2 * pairs, WAVES - 1 - 2 * pairs)):
        angles = (waves[:, None] * points[None, :] % NLON) * (2.0 * math.pi / NLON)
        tables[p, 0, :, :HALF] = np.cos(angles) / math.sqrt(NLON)
        tables[p, 1, :, :HALF] = -np.sin(angles) / math.sqrt(NLON)
    return tables.reshape(2, 2 * PAIRS, WIDE).astype(ml_dtypes.bfloat16)


def select8(index, values):
    result = jnp.int32(values[0])
    for k in range(1, len(values)):
        result = jnp.where(index == k, values[k], result)
    return result


Z_ORDER = (0, 1, 7, 2, 6, 3, 5, 4)
Y_ORDER = (0, 1, 3, 2)


def lev_offset(index):
    return select8(index % 4, Y_ORDER), index // 4


def lev_at(l, index):
    dx, dc = lev_offset(index)
    return (l // 2 + dx) % 4 * 2 + (l % 2 + dc) % 2


def lev_from(l, index):
    dx, dc = lev_offset(index)
    return (l // 2 + 4 - dx) % 4 * 2 + (l % 2 + dc) % 2


def wave_at(w, index):
    dz = select8(index % 8, Z_ORDER)
    dy = select8(index // 8, Y_ORDER)
    return (w // 4 + dz) % 8 * 4 + (w % 4 + dy) % 4


def sub_iota(shape):
    return lax.broadcasted_iota(jnp.int32, shape, len(shape) - 2)


def lane_iota(shape):
    return lax.broadcasted_iota(jnp.int32, shape, len(shape) - 1)


def swap_lane(a0, a1, a2, a3):
    lane = lane_iota(a0.shape)
    low64 = lane < 64
    low32 = lane % 64 < 32

    def roll(x, s):
        return pltpu.roll(x, s, 1)

    lo0 = jnp.where(low64, a0, roll(a2, 64))
    lo1 = jnp.where(low64, a1, roll(a3, 64))
    hi0 = jnp.where(low64, roll(a0, 64), a2)
    hi1 = jnp.where(low64, roll(a1, 64), a3)
    return (
        jnp.where(low32, lo0, roll(lo1, 32)),
        jnp.where(low32, roll(lo0, 96), lo1),
        jnp.where(low32, hi0, roll(hi1, 32)),
        jnp.where(low32, roll(hi0, 96), hi1),
    )


BLOCKS = [(2048, 128)] + [(256 * n, 256) for n in range(8)]


def exchange(
    field_hbm, leg_hbm, table_hbm, ids_hbm, weights_hbm, points_hbm, diffusion_hbm,
    spec, grid,
    field, raw, leg, last, table, fold, pairs, send_f, recv_f, oper, damp, dope, modes, send_b,
    recv_b, rows, turned, onehot, column, back, gat1, gat2, gatv, gats, ids, weights, points,
    diffusion,
    s_table, s_field, s_leg, s_local, s_small, s_g1s, s_g1r, s_g2s, s_g2r, s_fs, s_fr, s_bs, s_br,
):
    w = lax.axis_index("wave")
    l = lax.axis_index("lev")
    me = w * NLEV + l

    small_copies = [
        pltpu.make_async_copy(a, b, s_small.at[i])
        for i, (a, b) in enumerate((
            (ids_hbm, ids), (weights_hbm, weights), (points_hbm, points), (diffusion_hbm, diffusion),
        ))
    ]
    for copy in small_copies:
        copy.start()
    field_copy = pltpu.make_async_copy(field_hbm, field, s_field)
    field_copy.start()
    table_copies = [
        pltpu.make_async_copy(table_hbm.at[p], table.at[p], s_table.at[p]) for p in range(2)
    ]
    table_copies[0].start()
    leg_copy = pltpu.make_async_copy(leg_hbm, raw, s_leg)

    barrier = pltpu.get_barrier_semaphore()

    def greet_lev(i, c):
        pl.semaphore_signal(barrier, inc=1, device_id=(w, (l + i) % NLEV), device_id_type=MESH)
        return c

    def greet_wave(i, c):
        pl.semaphore_signal(barrier, inc=1, device_id=((w + i) % NWAVE, l), device_id_type=MESH)
        return c

    lax.fori_loop(1, NLEV, greet_lev, 0)
    lax.fori_loop(1, NWAVE, greet_wave, 0)

    for copy in small_copies:
        copy.wait()
    a0 = ids[0]
    a1 = ids[1]
    t0 = jnp.where(a0 % 2 == 0, a0 // 2, (WAVES - 1 - a0) // 2)
    t1 = jnp.where(a1 % 2 == 0, a1 // 2, (WAVES - 1 - a1) // 2)
    flat = sub_iota((8, 128)) * 128 + lane_iota((8, 128))
    tile = jnp.where(flat == 2 * me, t0, 0) + jnp.where(flat == 2 * me + 1, t1, 0)
    tile = tile + jnp.where(flat == PAIRS + t0, 2 * me, 0)
    tile = tile + jnp.where(flat == PAIRS + t1, 2 * me + 1, 0)
    gat1[l] = tile

    band = pl.multiple_of(w // 4 * 128, 128)
    turn = (4 - w % 4) % 4 * 32
    lane1 = lane_iota((8, 128))

    def spread(row):
        moved = pltpu.roll(jnp.broadcast_to(row, (8, 128)), turn, 1)
        first = jnp.where(lane1 < 32, moved, jnp.zeros_like(moved))
        twice = first + pltpu.roll(first, 32, 1)
        return twice + pltpu.roll(twice, 64, 1)

    band_weights = spread(weights[:, pl.ds(band, 128)])
    band_points = [spread(points[h:h + 1, pl.ds(band, 128)]) for h in range(2)]

    pl.semaphore_wait(barrier, NLEV - 1 + NWAVE - 1)

    def send_g1(i, c):
        pltpu.make_async_remote_copy(
            src_ref=gat1.at[l], dst_ref=gat1.at[l], send_sem=s_g1s, recv_sem=s_g1r,
            device_id=(w, (l + i) % NLEV), device_id_type=MESH,
        ).start()
        return c

    lax.fori_loop(1, NLEV, send_g1, 0)

    field_copy.wait()
    table_copies[1].start()

    def fold_body(i, c):
        f = i // 4
        h = i // 2 % 2
        j = pl.multiple_of(i % 2 * 16, 16)
        first = field[f, h, pl.ds(j, 16), 0:WIDE].astype(F32)
        second = field[f, h, pl.ds(j, 16), NLON - WIDE:NLON].astype(F32)
        second = pltpu.roll(second, HALF, 1)
        row = pl.multiple_of(h * 128 + f * 32 + j, 16)
        fold[0, pl.ds(row, 16), :] = (first + second).astype(BF16)
        fold[1, pl.ds(row, 16), :] = (first - second).astype(BF16)
        return c

    lax.fori_loop(0, 16, fold_body, 0)

    g1 = pltpu.make_async_remote_copy(
        src_ref=gat1.at[pl.ds(0, NLEV - 1)], dst_ref=gat1.at[pl.ds(0, NLEV - 1)], send_sem=s_g1s,
        recv_sem=s_g1r, device_id=(w, l), device_id_type=MESH,
    )
    g1.wait_send()
    g1.wait_recv()
    total = gat1[0]
    for i in range(1, NLEV):
        total = total + gat1[i]
    gat2[w] = total

    def send_g2(i, c):
        pltpu.make_async_remote_copy(
            src_ref=gat2.at[w], dst_ref=gat2.at[w], send_sem=s_g2s, recv_sem=s_g2r,
            device_id=((w + i) % NWAVE, l), device_id_type=MESH,
        ).start()
        return c

    lax.fori_loop(1, NWAVE, send_g2, 0)

    def twice_wave(p, pair):
        return 4 * pair if p == 0 else 2 * (WAVES - 1) - 4 * pair

    def transform(p):
        def body(part, c):
            start = pl.multiple_of(part * PAIRS, PAIRS)
            out = lax.dot_general(
                table[p, pl.ds(start, PAIRS), :], fold[p], NT, preferred_element_type=F32
            )
            twice = twice_wave(p, sub_iota((PAIRS, 128)))
            north = jnp.where(twice < band_points[0][0:1, :], out[:, :128], 0.0)
            south = jnp.where(twice < band_points[1][0:1, :], out[:, 128:], 0.0)
            scale = band_weights[0:1, :]
            pairs[:, 2 * p + part, :] = (north + south) * scale
            pairs[:, 4 + 2 * p + part, :] = (north - south) * scale
            return c

        lax.fori_loop(0, 2, body, 0)

    table_copies[0].wait()
    transform(0)
    table_copies[1].wait()
    leg_copy.start()
    transform(1)

    g2 = pltpu.make_async_remote_copy(
        src_ref=gat2.at[pl.ds(0, NWAVE - 1)], dst_ref=gat2.at[pl.ds(0, NWAVE - 1)], send_sem=s_g2s,
        recv_sem=s_g2r, device_id=(w, l), device_id_type=MESH,
    )
    g2.wait_send()
    g2.wait_recv()
    total = gat2[0]
    for i in range(1, NWAVE):
        total = total + gat2[i]
    gatv[...] = jnp.clip(total, 0, PAIRS - 1)
    ids_copy = pltpu.make_async_copy(gatv, gats, s_local)
    ids_copy.start()
    ids_copy.wait()

    def packed(d):
        first = gats[d // 64, 2 * d % 128]
        second = gats[d // 64, 2 * d % 128 + 1]
        return jnp.concatenate([pairs[first], pairs[second]], axis=0).astype(BF16)

    recv_f[me] = packed(me)

    def send_forward(i, c):
        j = 256 - i
        w2 = wave_at(w, j % NWAVE)
        l2 = lev_at(l, j // NWAVE)
        d = w2 * NLEV + l2
        send_f[d] = packed(d)
        pltpu.make_async_remote_copy(
            src_ref=send_f.at[d], dst_ref=recv_f.at[me], send_sem=s_fs, recv_sem=s_fr.at[l],
            device_id=(w2, l2), device_id_type=MESH,
        ).start()
        return c

    lax.fori_loop(1, 256, send_forward, 0, unroll=5)

    leg_copy.wait()

    def relay(i, c):
        k = pl.multiple_of(i * 16, 16)
        for ch in range(8):
            x = raw[pl.ds(k, 16), ch].astype(F32)
            for s in range(2):
                leg[s, pl.ds(k, 16), ch * 128:(ch + 1) * 128] = x[:, s, :].astype(BF16)
        return c

    lax.fori_loop(0, 64, relay, 0)
    for ch in range(8):
        x = raw[1024, ch].astype(F32)
        for s in range(2):
            last[s, :, ch * 128:(ch + 1) * 128] = jnp.broadcast_to(x[s:s + 1], (16, 128)).astype(BF16)

    def field_of(g):
        core = (l + 1 + g // 16) % 2
        return (g // 4 % 4 * 2 + core) * 4 + g % 4

    def chosen(a, base, width):
        sub = sub_iota((8, width))
        k = base + lane_iota((8, width))
        is_a = k < WAVES - a
        parity = jnp.where(is_a, k % 2, (k + a) % 2)
        member = jnp.where(is_a, a % 2, 1 - a % 2)
        sel = (sub // 4 == parity) & (sub // 2 % 2 == member) & (k < ROWS)
        degree = jnp.where(is_a, a + k, k - 1)
        return sel, degree

    for s, a in enumerate((a0, a1)):
        sel, degree = chosen(a, 0, ROWP)
        level = degree.astype(F32)
        scaled = level * (level + 1.0) / (WAVES * (WAVES - 1.0))
        squared = scaled * scaled
        one = jnp.where(sel, 1.0, 0.0)

        def damp_body(f, c, s=s, squared=squared, one=one):
            row = pl.multiple_of(f * 8, 8)
            damp[s, pl.ds(row, 8), :] = one / (1.0 + diffusion[field_of(f)] * squared)
            return c

        lax.fori_loop(0, 32, damp_body, 0)

    for q in range(4):
        bases = [2 * lev_from(l, 7 - 2 * q - u) for u in range(2)]

        def onehot_body(b, c, q=q, bases=bases):
            sub = sub_iota((128, 128))
            slot = jnp.where(sub < 64, bases[0], bases[1]) + sub % 64 // 2 * 16 + sub % 2
            for b in range(4):
                hit = slot == gatv[4 + b:5 + b, :]
                onehot[q * 128:(q + 1) * 128, b * 128:(b + 1) * 128] = jnp.where(
                    hit, 1.0, 0.0
                ).astype(BF16)
            return c

        lax.fori_loop(0, 1, onehot_body, 0)
    for h in range(2):
        column[h] = jnp.broadcast_to(band_points[h][0:1, :].astype(F32), (128, 128)).T

    def arrive(i, c):
        src = lev_from(l, 7 - i)

        def landed(count):
            pltpu.make_async_remote_copy(
                src_ref=send_f.at[pl.ds(0, count)], dst_ref=recv_f.at[pl.ds(0, count)],
                send_sem=s_fs, recv_sem=s_fr.at[src], device_id=(w, l), device_id_type=MESH,
            ).wait_recv()

        @pl.when(src == l)
        def _():
            landed(NWAVE - 1)

        @pl.when(src != l)
        def _():
            landed(NWAVE)

        for block in range(8):
            tiles = [recv_f[(4 * block + v) * NLEV + src].astype(F32) for v in range(4)]
            by_field = swap_lane(*tiles)
            for s in range(2):
                for pair in range(2):
                    row = pl.multiple_of(i // 4 * 128 + src // 2 * 32 + pair * 16, 16)
                    oper[s, pl.ds(row, 16), block * 128:(block + 1) * 128] = jnp.concatenate(
                        [
                            by_field[2 * pair][8 * s:8 * s + 8],
                            by_field[2 * pair + 1][8 * s:8 * s + 8],
                        ],
                        axis=0,
                    ).astype(BF16)
        return c

    def pick(half, s, a, x, start, width):
        sel, _ = chosen(a, start, width)
        lanes = pl.ds(start, width)
        for i in range(8):
            damped = []
            for g in (2 * i, 2 * i + 1):
                y = jnp.where(sel, x[8 * g:8 * g + 8], 0.0)
                y = y + pltpu.roll(y, 4, 0)
                y = y + pltpu.roll(y, 2, 0)
                f = field_of(16 * half + g)
                if width == 128:
                    spec[s, f, :, 1024:ROWS] = y[0:2, 0:1]
                else:
                    spec[s, f, :, lanes] = y[0:2]
                row = 128 * half + 8 * g
                damped.append(y * damp[s, row:row + 8, lanes])
            row = 128 * half + 16 * i
            dope[s, row:row + 16, lanes] = jnp.concatenate(damped, axis=0).astype(BF16)

    def legendre_step(half):
        mine = slice(128 * half, 128 * half + 128)

        def product(n, c):
            start = pl.multiple_of(n * 256, 256)
            for s, a in enumerate((a0, a1)):
                x = lax.dot_general(
                    oper[s, mine], leg[s, pl.ds(start, 256), :], NT, preferred_element_type=F32
                )
                pick(half, s, a, x, start, 256)
            return c

        lax.fori_loop(0, 4, product, 0, unroll=2)
        for s, a in enumerate((a0, a1)):
            rhs = jnp.concatenate([last[s]] * 8, axis=0)
            x = lax.dot_general(oper[s, mine], rhs, NT, preferred_element_type=F32)
            pick(half, s, a, x, 1024, 128)

        def inverse(n, c):
            start = pl.multiple_of(n * 256, 256)
            sign = jnp.where(sub_iota((1, 8, 256)) < 4, 1.0, -1.0)
            for s in range(2):
                x = lax.dot_general(
                    dope[s, mine, 0:1024], leg[s, 0:1024, pl.ds(start, 256)], NN,
                    preferred_element_type=F32,
                )
                edge = dope[s, mine, 1024:ROWP].astype(F32)[:, 0:1]
                x = x + edge * last[s, :, pl.ds(start, 256)].astype(F32)[0:1]
                x = x.reshape(16, 8, 256)
                modes[s, 16 * half:16 * half + 16, :, pl.ds(start, 256)] = (
                    x * sign + pltpu.roll(x, 4, 1)
                )
            return c

        lax.fori_loop(0, 4, inverse, 0, unroll=2)

    def send_group(i, c):
        l2 = lev_at(l, 7 - i)
        for block in range(8):
            lanes = slice(block * 128, (block + 1) * 128)
            tiles = [
                jnp.concatenate([modes[s, i // 4 * 16 + l2 // 2 * 4 + f, :, lanes] for s in range(2)], axis=0)
                for f in range(4)
            ]
            for u, x in enumerate(swap_lane(*tiles)):
                send_b[(4 * block + u) * NLEV + l2] = x.astype(BF16)

        def send_back(m, c):
            w2 = wave_at(w, 31 - m)
            d = w2 * NLEV + l2

            @pl.when(d != me)
            def _():
                pltpu.make_async_remote_copy(
                    src_ref=send_b.at[d], dst_ref=recv_b.at[me], send_sem=s_bs,
                    recv_sem=s_br.at[l], device_id=(w2, l2), device_id_type=MESH,
                ).start()

            return c

        lax.fori_loop(0, 32, send_back, 0)
        return c

    for half in range(2):
        lax.fori_loop(4 * half, 4 * half + 4, arrive, 0)
        legendre_step(half)
        lax.fori_loop(4 * half, 4 * half + 4, send_group, 0)
    recv_b[me] = send_b[me]

    def returned(q, c):
        for u in range(2):
            src = lev_from(l, 7 - 2 * q - u)

            def landed(count, src=src):
                pltpu.make_async_remote_copy(
                    src_ref=send_b.at[pl.ds(0, count)], dst_ref=recv_b.at[pl.ds(0, count)],
                    send_sem=s_bs, recv_sem=s_br.at[src], device_id=(w, l), device_id_type=MESH,
                ).wait_recv()

            @pl.when(src == l)
            def _():
                landed(NWAVE - 1)

            @pl.when(src != l)
            def _():
                landed(NWAVE)

            for v in range(NWAVE):
                both = recv_b[v * NLEV + src].astype(F32)
                rows[64 * u + 2 * v] = both[0:8]
                rows[64 * u + 2 * v + 1] = both[8:16]
        lanes = pl.multiple_of(q * 128, 128)
        for j in range(8):
            turned[j, :, pl.ds(lanes, 128)] = rows[:, j, :].T.astype(BF16)
        return c

    lax.fori_loop(0, 4, returned, 0)

    for h in range(2):
        for p in range(2):
            for r in range(2):
                x = lax.dot_general(
                    turned[4 * h + 2 * p + r], onehot[...], NN, preferred_element_type=F32
                )
                limit = jnp.concatenate([column[h]] * 4, axis=1)
                twice = twice_wave(p, lane_iota((128, PAIRS)))
                x = jnp.where(twice.astype(F32) < limit, x, 0.0)
                x = x * (jnp.where(twice == 0, 1.0, 2.0) if p == 0 else 2.0)
                back[p, h * 128:(h + 1) * 128, r * PAIRS:(r + 1) * PAIRS] = x.astype(BF16)

    def write(x, start, width):
        for h in range(2):
            for f in range(4):
                row = h * 128 + f * 32
                grid[f, h, :, start:start + width] = x[row:row + 32].astype(BF16)

    tail = None
    before = None
    for start, width in BLOCKS:
        x = jnp.dot(back[0], table[0, :, start:start + width], preferred_element_type=F32)
        y = jnp.dot(back[1], table[1, :, start:start + width], preferred_element_type=F32)
        total = x + y
        differ = pltpu.roll(x - y, 64, 1)
        if width == 128:
            tail = differ
            before = total
        else:
            low = lane_iota((256, 128)) < 64
            write(total, start, 256)
            edge = jnp.where(low, before, differ[:, :128])
            write(jnp.concatenate([edge, differ[:, 128:]], axis=1), 2048 + start, 256)
            before = differ[:, :128]
    write(jnp.where(lane_iota((256, 128)) < 64, before, tail), 4096, 128)

    pltpu.make_async_remote_copy(
        src_ref=send_f.at[pl.ds(0, 255)], dst_ref=recv_f.at[pl.ds(0, 255)], send_sem=s_fs,
        recv_sem=s_g1r, device_id=(w, l), device_id_type=MESH,
    ).wait_send()
    pltpu.make_async_remote_copy(
        src_ref=send_b.at[pl.ds(0, 255)], dst_ref=recv_b.at[pl.ds(0, 255)], send_sem=s_bs,
        recv_sem=s_g1r, device_id=(w, l), device_id_type=MESH,
    ).wait_send()


def shards(grid_field, legendre, wave_groups, lat_weights, cycle_points, diffusion):
    dma = pltpu.SemaphoreType.DMA
    vmem = pl.BlockSpec(memory_space=pltpu.VMEM)
    hbm = pl.BlockSpec(memory_space=pltpu.HBM)
    table = jnp.asarray(basis_tables())
    by_row = legendre.reshape(2, ROWS, 8, 128).transpose(1, 2, 0, 3)
    return pl.pallas_call(
        exchange,
        out_shape=(
            pltpu.VMEM((2, 32, 2, ROWS), F32),
            pltpu.VMEM((4, 2, 32, NLON), BF16),
        ),
        in_specs=[hbm] * 7,
        out_specs=(vmem, vmem),
        scratch_shapes=[
            pltpu.VMEM((4, 2, 32, NLON), BF16),
            pltpu.VMEM((ROWS, 8, 2, 128), BF16),
            pltpu.VMEM((2, 1024, 1024), BF16),
            pltpu.VMEM((2, 16, 1024), BF16),
            pltpu.VMEM((2, 1024, WIDE), BF16),
            pltpu.VMEM((2, 256, WIDE), BF16),
            pltpu.VMEM((PAIRS, 8, 128), F32),
            pltpu.VMEM((256, 16, 128), BF16),
            pltpu.VMEM((256, 16, 128), BF16),
            pltpu.VMEM((2, 256, 1024), BF16),
            pltpu.VMEM((2, 256, ROWP), F32),
            pltpu.VMEM((2, 256, ROWP), BF16),
            pltpu.VMEM((2, 32, 8, 1024), F32),
            pltpu.VMEM((256, 16, 128), BF16),
            pltpu.VMEM((256, 16, 128), BF16),
            pltpu.VMEM((128, 8, 128), F32),
            pltpu.VMEM((8, 128, PAIRS), BF16),
            pltpu.VMEM((PAIRS, PAIRS), BF16),
            pltpu.VMEM((2, 128, 128), F32),
            pltpu.VMEM((2, 256, 1024), BF16),
            pltpu.VMEM((NLEV, 8, 128), jnp.int32),
            pltpu.VMEM((NWAVE, 8, 128), jnp.int32),
            pltpu.VMEM((8, 128), jnp.int32),
            pltpu.SMEM((8, 128), jnp.int32),
            pltpu.SMEM((2,), jnp.int32),
            pltpu.VMEM((1, 1024), F32),
            pltpu.VMEM((2, 1024), jnp.int32),
            pltpu.SMEM((32,), F32),
            dma((2,)), dma, dma, dma, dma((4,)), dma, dma, dma, dma, dma, dma((NLEV,)), dma,
            dma((NLEV,)),
        ],
        compiler_params=pltpu.CompilerParams(
            collective_id=0, has_side_effects=True, vmem_limit_bytes=56 << 20
        ),
        name="exchange",
    )(grid_field, by_row, table, wave_groups, lat_weights.reshape(1, -1), cycle_points, diffusion)


def solution(mesh):
    return jax.shard_map(
        shards,
        mesh=mesh,
        in_specs=(
            P("lev", None, "wave", None),
            P(("wave", "lev"), None, None),
            P(("wave", "lev")),
            P(),
            P(),
            P(),
        ),
        out_specs=(P(("wave", "lev"), None, None, None), P("lev", None, "wave", None)),
        check_vma=False,
    )
```

```python
import math

import jax
import jax.numpy as jnp
import ml_dtypes
import numpy as np
from jax import lax
from jax.experimental import pallas as pl
from jax.experimental.pallas import tpu as pltpu
from jax.sharding import PartitionSpec as P

WAVES = 1024
PAIRS = 512
NLON = 4224
HALF = NLON // 2
WIDE = 2176
ROWS = 1025
ROWP = 1152
NWAVE = 32
NLEV = 8
MESH = pl.DeviceIdType.MESH
F32 = jnp.float32
BF16 = jnp.bfloat16
NT = (((1,), (1,)), ((), ()))
NN = (((1,), (0,)), ((), ()))


def basis_tables():
    pairs = np.arange(PAIRS, dtype=np.int64)
    points = np.arange(HALF, dtype=np.int64)
    tables = np.zeros((2, 2, PAIRS, WIDE), np.float32)
    for p, waves in enumerate((2 * pairs, WAVES - 1 - 2 * pairs)):
        angles = (waves[:, None] * points[None, :] % NLON) * (2.0 * math.pi / NLON)
        tables[p, 0, :, :HALF] = np.cos(angles) / math.sqrt(NLON)
        tables[p, 1, :, :HALF] = -np.sin(angles) / math.sqrt(NLON)
    return tables.reshape(2, 2 * PAIRS, WIDE).astype(ml_dtypes.bfloat16)


def select8(index, values):
    result = jnp.int32(values[0])
    for k in range(1, len(values)):
        result = jnp.where(index == k, values[k], result)
    return result


Z_ORDER = (0, 1, 7, 2, 6, 3, 5, 4)
Y_ORDER = (0, 1, 3, 2)


def lev_offset(index):
    return select8(index % 4, Y_ORDER), index // 4


def lev_at(l, index):
    dx, dc = lev_offset(index)
    return (l // 2 + dx) % 4 * 2 + (l % 2 + dc) % 2


def lev_from(l, index):
    dx, dc = lev_offset(index)
    return (l // 2 + 4 - dx) % 4 * 2 + (l % 2 + dc) % 2


def wave_at(w, index):
    dz = select8(index % 8, Z_ORDER)
    dy = select8(index // 8, Y_ORDER)
    return (w // 4 + dz) % 8 * 4 + (w % 4 + dy) % 4


def sub_iota(shape):
    return lax.broadcasted_iota(jnp.int32, shape, len(shape) - 2)


def lane_iota(shape):
    return lax.broadcasted_iota(jnp.int32, shape, len(shape) - 1)


def swap_lane(a0, a1, a2, a3):
    lane = lane_iota(a0.shape)
    low64 = lane < 64
    low32 = lane % 64 < 32

    def roll(x, s):
        return pltpu.roll(x, s, 1)

    lo0 = jnp.where(low64, a0, roll(a2, 64))
    lo1 = jnp.where(low64, a1, roll(a3, 64))
    hi0 = jnp.where(low64, roll(a0, 64), a2)
    hi1 = jnp.where(low64, roll(a1, 64), a3)
    return (
        jnp.where(low32, lo0, roll(lo1, 32)),
        jnp.where(low32, roll(lo0, 96), lo1),
        jnp.where(low32, hi0, roll(hi1, 32)),
        jnp.where(low32, roll(hi0, 96), hi1),
    )


BLOCKS = [(2048, 128)] + [(256 * n, 256) for n in range(8)]


def exchange(
    field_hbm, leg_hbm, table_hbm, ids_hbm, weights_hbm, points_hbm, diffusion_hbm,
    spec, grid,
    field, raw, leg, last, table, fold, pairs, send_f, recv_f, oper, damp, dope, modes, send_b,
    recv_b, rows, turned, onehot, column, back, gat1, gat2, gatv, gats, ids, weights, points,
    diffusion,
    s_table, s_field, s_leg, s_local, s_small, s_g1s, s_g1r, s_g2s, s_g2r, s_fs, s_fr, s_bs, s_br,
):
    w = lax.axis_index("wave")
    l = lax.axis_index("lev")
    me = w * NLEV + l

    small_copies = [
        pltpu.make_async_copy(a, b, s_small.at[i])
        for i, (a, b) in enumerate((
            (ids_hbm, ids), (weights_hbm, weights), (points_hbm, points), (diffusion_hbm, diffusion),
        ))
    ]
    for copy in small_copies:
        copy.start()
    field_copy = pltpu.make_async_copy(field_hbm, field, s_field)
    field_copy.start()
    table_copies = [
        pltpu.make_async_copy(table_hbm.at[p], table.at[p], s_table.at[p]) for p in range(2)
    ]
    leg_copy = pltpu.make_async_copy(leg_hbm, raw, s_leg)

    barrier = pltpu.get_barrier_semaphore()

    def greet_lev(i, c):
        pl.semaphore_signal(barrier, inc=1, device_id=(w, (l + i) % NLEV), device_id_type=MESH)
        return c

    def greet_wave(i, c):
        pl.semaphore_signal(barrier, inc=1, device_id=((w + i) % NWAVE, l), device_id_type=MESH)
        return c

    lax.fori_loop(1, NLEV, greet_lev, 0)
    lax.fori_loop(1, NWAVE, greet_wave, 0)
    table_copies[0].start()

    for copy in small_copies:
        copy.wait()
    a0 = ids[0]
    a1 = ids[1]
    t0 = jnp.where(a0 % 2 == 0, a0 // 2, (WAVES - 1 - a0) // 2)
    t1 = jnp.where(a1 % 2 == 0, a1 // 2, (WAVES - 1 - a1) // 2)
    lane = lane_iota((1, 128))
    place = 2 * me % 128
    gat1[l] = jnp.where(lane == place, t0, 0) + jnp.where(lane == place + 1, t1, 0)

    band = pl.multiple_of(w // 4 * 128, 128)
    turn = (4 - w % 4) % 4 * 32
    lane1 = lane_iota((8, 128))

    def spread(row):
        moved = pltpu.roll(jnp.broadcast_to(row, (8, 128)), turn, 1)
        first = jnp.where(lane1 < 32, moved, jnp.zeros_like(moved))
        twice = first + pltpu.roll(first, 32, 1)
        return twice + pltpu.roll(twice, 64, 1)

    band_weights = spread(weights[:, pl.ds(band, 128)])
    band_points = [spread(points[h:h + 1, pl.ds(band, 128)]) for h in range(2)]

    pl.semaphore_wait(barrier, NLEV - 1 + NWAVE - 1)

    def send_g1(i, c):
        pltpu.make_async_remote_copy(
            src_ref=gat1.at[l], dst_ref=gat1.at[l], send_sem=s_g1s, recv_sem=s_g1r,
            device_id=(w, (l + i) % NLEV), device_id_type=MESH,
        ).start()
        return c

    lax.fori_loop(1, NLEV, send_g1, 0)

    field_copy.wait()
    table_copies[1].start()

    def fold_body(i, c):
        f = i // 4
        h = i // 2 % 2
        j = pl.multiple_of(i % 2 * 16, 16)
        first = field[f, h, pl.ds(j, 16), 0:WIDE].astype(F32)
        second = field[f, h, pl.ds(j, 16), NLON - WIDE:NLON].astype(F32)
        second = pltpu.roll(second, HALF, 1)
        row = pl.multiple_of(h * 128 + f * 32 + j, 16)
        fold[0, pl.ds(row, 16), :] = (first + second).astype(BF16)
        fold[1, pl.ds(row, 16), :] = (first - second).astype(BF16)
        return c

    lax.fori_loop(0, 16, fold_body, 0)

    g1 = pltpu.make_async_remote_copy(
        src_ref=gat1.at[pl.ds(0, NLEV - 1)], dst_ref=gat1.at[pl.ds(0, NLEV - 1)], send_sem=s_g1s,
        recv_sem=s_g1r, device_id=(w, l), device_id_type=MESH,
    )
    g1.wait_send()
    g1.wait_recv()
    total = gat1[0]
    for i in range(1, NLEV):
        total = total + gat1[i]
    gat2[w] = total

    def send_g2(i, c):
        pltpu.make_async_remote_copy(
            src_ref=gat2.at[w], dst_ref=gat2.at[w], send_sem=s_g2s, recv_sem=s_g2r,
            device_id=((w + i) % NWAVE, l), device_id_type=MESH,
        ).start()
        return c

    lax.fori_loop(1, NWAVE, send_g2, 0)

    def twice_wave(p, pair):
        return 4 * pair if p == 0 else 2 * (WAVES - 1) - 4 * pair

    def transform(p):
        def body(part, c):
            start = pl.multiple_of(part * PAIRS, PAIRS)
            out = lax.dot_general(
                table[p, pl.ds(start, PAIRS), :], fold[p], NT, preferred_element_type=F32
            )
            twice = twice_wave(p, sub_iota((PAIRS, 128)))
            north = jnp.where(twice < band_points[0][0:1, :], out[:, :128], 0.0)
            south = jnp.where(twice < band_points[1][0:1, :], out[:, 128:], 0.0)
            scale = band_weights[0:1, :]
            pairs[:, 2 * p + part, :] = (north + south) * scale
            pairs[:, 4 + 2 * p + part, :] = (north - south) * scale
            return c

        lax.fori_loop(0, 2, body, 0, unroll=2)

    table_copies[0].wait()
    transform(0)
    table_copies[1].wait()
    leg_copy.start()
    transform(1)

    g2 = pltpu.make_async_remote_copy(
        src_ref=gat2.at[pl.ds(0, NWAVE - 1)], dst_ref=gat2.at[pl.ds(0, NWAVE - 1)], send_sem=s_g2s,
        recv_sem=s_g2r, device_id=(w, l), device_id_type=MESH,
    )
    g2.wait_send()
    g2.wait_recv()
    for r in range(4):
        total = gat2[8 * r]
        for i in range(1, 8):
            total = total + gat2[8 * r + i]
        gatv[r:r + 1, :] = jnp.clip(total, 0, PAIRS - 1)
    ids_copy = pltpu.make_async_copy(gatv, gats, s_local)
    ids_copy.start()
    ids_copy.wait()

    def packed(d):
        first = gats[d // 64, 2 * d % 128]
        second = gats[d // 64, 2 * d % 128 + 1]
        return jnp.concatenate([pairs[first], pairs[second]], axis=0).astype(BF16)

    recv_f[me] = packed(me)

    def send_forward(i, c):
        j = 256 - i
        w2 = wave_at(w, j % NWAVE)
        l2 = lev_at(l, j // NWAVE)
        d = w2 * NLEV + l2
        send_f[d] = packed(d)
        pltpu.make_async_remote_copy(
            src_ref=send_f.at[d], dst_ref=recv_f.at[me], send_sem=s_fs, recv_sem=s_fr.at[l],
            device_id=(w2, l2), device_id_type=MESH,
        ).start()
        return c

    lax.fori_loop(1, 256, send_forward, 0, unroll=5)

    leg_copy.wait()

    def relay(i, c):
        k = pl.multiple_of(i * 16, 16)
        for ch in range(8):
            x = raw[pl.ds(k, 16), ch].astype(F32)
            for s in range(2):
                leg[s, pl.ds(k, 16), ch * 128:(ch + 1) * 128] = x[:, s, :].astype(BF16)
        return c

    lax.fori_loop(0, 64, relay, 0)
    for ch in range(8):
        x = raw[1024, ch].astype(F32)
        for s in range(2):
            last[s, :, ch * 128:(ch + 1) * 128] = jnp.broadcast_to(x[s:s + 1], (16, 128)).astype(BF16)

    def field_of(g):
        core = (l + 1 + g // 16) % 2
        return (g // 4 % 4 * 2 + core) * 4 + g % 4

    def chosen(a, base, width):
        sub = sub_iota((8, width))
        k = base + lane_iota((8, width))
        is_a = k < WAVES - a
        parity = jnp.where(is_a, k % 2, (k + a) % 2)
        member = jnp.where(is_a, a % 2, 1 - a % 2)
        sel = (sub // 4 == parity) & (sub // 2 % 2 == member) & (k < ROWS)
        degree = jnp.where(is_a, a + k, k - 1)
        return sel, degree

    for s, a in enumerate((a0, a1)):
        sel, degree = chosen(a, 0, ROWP)
        level = degree.astype(F32)
        scaled = level * (level + 1.0) / (WAVES * (WAVES - 1.0))
        squared = scaled * scaled
        one = jnp.where(sel, 1.0, 0.0)

        def damp_body(f, c, s=s, squared=squared, one=one):
            row = pl.multiple_of(f * 8, 8)
            damp[s, pl.ds(row, 8), :] = one / (1.0 + diffusion[field_of(f)] * squared)
            return c

        lax.fori_loop(0, 32, damp_body, 0)

    holders = [jnp.zeros((1, 128), F32)] * 4
    for r in range(4):
        held = jnp.broadcast_to(gatv[r:r + 1, :].astype(F32), (128, 128)).T
        slot = (128 * r + sub_iota((128, 128))).astype(F32)
        for b in range(4):
            pair = (128 * b + lane_iota((128, 128))).astype(F32)
            hit = jnp.where(held == pair, slot, 0.0)
            holders[b] = holders[b] + jnp.sum(hit, axis=0, keepdims=True)
    holders = [holder.astype(jnp.int32) for holder in holders]

    for q in range(4):
        bases = [2 * lev_from(l, 7 - 2 * q - u) for u in range(2)]

        def onehot_body(b, c, q=q, bases=bases):
            sub = sub_iota((128, 128))
            slot = jnp.where(sub < 64, bases[0], bases[1]) + sub % 64 // 2 * 16 + sub % 2
            for b in range(4):
                hit = slot == holders[b]
                onehot[q * 128:(q + 1) * 128, b * 128:(b + 1) * 128] = jnp.where(
                    hit, 1.0, 0.0
                ).astype(BF16)
            return c

        lax.fori_loop(0, 1, onehot_body, 0)
    for h in range(2):
        column[h] = jnp.broadcast_to(band_points[h][0:1, :].astype(F32), (128, 128)).T

    def arrive(i, c):
        src = lev_from(l, 7 - i)

        def landed(count):
            pltpu.make_async_remote_copy(
                src_ref=send_f.at[pl.ds(0, count)], dst_ref=recv_f.at[pl.ds(0, count)],
                send_sem=s_fs, recv_sem=s_fr.at[src], device_id=(w, l), device_id_type=MESH,
            ).wait_recv()

        @pl.when(src == l)
        def _():
            landed(NWAVE - 1)

        @pl.when(src != l)
        def _():
            landed(NWAVE)

        for block in range(8):
            tiles = [recv_f[(4 * block + v) * NLEV + src].astype(F32) for v in range(4)]
            by_field = swap_lane(*tiles)
            for s in range(2):
                for pair in range(2):
                    row = pl.multiple_of(i // 4 * 128 + src // 2 * 32 + pair * 16, 16)
                    oper[s, pl.ds(row, 16), block * 128:(block + 1) * 128] = jnp.concatenate(
                        [
                            by_field[2 * pair][8 * s:8 * s + 8],
                            by_field[2 * pair + 1][8 * s:8 * s + 8],
                        ],
                        axis=0,
                    ).astype(BF16)
        return c

    def pick(half, s, a, x, start, width):
        sel, _ = chosen(a, start, width)
        lanes = pl.ds(start, width)
        for i in range(8):
            damped = []
            for g in (2 * i, 2 * i + 1):
                y = jnp.where(sel, x[8 * g:8 * g + 8], 0.0)
                y = y + pltpu.roll(y, 4, 0)
                y = y + pltpu.roll(y, 2, 0)
                f = field_of(16 * half + g)
                if width == 128:
                    spec[s, f, :, 1024:ROWS] = y[0:2, 0:1]
                else:
                    spec[s, f, :, lanes] = y[0:2]
                row = 128 * half + 8 * g
                damped.append(y * damp[s, row:row + 8, lanes])
            row = 128 * half + 16 * i
            dope[s, row:row + 16, lanes] = jnp.concatenate(damped, axis=0).astype(BF16)

    def legendre_step(half):
        mine = slice(128 * half, 128 * half + 128)

        def product(n, c):
            start = pl.multiple_of(n * 256, 256)
            for s, a in enumerate((a0, a1)):
                x = lax.dot_general(
                    oper[s, mine], leg[s, pl.ds(start, 256), :], NT, preferred_element_type=F32
                )
                pick(half, s, a, x, start, 256)
            return c

        lax.fori_loop(0, 4, product, 0, unroll=2)
        for s, a in enumerate((a0, a1)):
            rhs = jnp.concatenate([last[s]] * 8, axis=0)
            x = lax.dot_general(oper[s, mine], rhs, NT, preferred_element_type=F32)
            pick(half, s, a, x, 1024, 128)

        def inverse(n, c):
            start = pl.multiple_of(n * 256, 256)
            sign = jnp.where(sub_iota((1, 8, 256)) < 4, 1.0, -1.0)
            for s in range(2):
                x = lax.dot_general(
                    dope[s, mine, 0:1024], leg[s, 0:1024, pl.ds(start, 256)], NN,
                    preferred_element_type=F32,
                )
                edge = dope[s, mine, 1024:ROWP].astype(F32)[:, 0:1]
                x = x + edge * last[s, :, pl.ds(start, 256)].astype(F32)[0:1]
                x = x.reshape(16, 8, 256)
                modes[s, 16 * half:16 * half + 16, :, pl.ds(start, 256)] = (
                    x * sign + pltpu.roll(x, 4, 1)
                )
            return c

        lax.fori_loop(0, 4, inverse, 0, unroll=2)

    def send_group(i, c):
        l2 = lev_at(l, 7 - i)
        for block in range(8):
            lanes = slice(block * 128, (block + 1) * 128)
            tiles = [
                jnp.concatenate([modes[s, i // 4 * 16 + l2 // 2 * 4 + f, :, lanes] for s in range(2)], axis=0)
                for f in range(4)
            ]
            for u, x in enumerate(swap_lane(*tiles)):
                send_b[(4 * block + u) * NLEV + l2] = x.astype(BF16)

        def send_back(m, c):
            w2 = wave_at(w, 31 - m)
            d = w2 * NLEV + l2

            @pl.when(d != me)
            def _():
                pltpu.make_async_remote_copy(
                    src_ref=send_b.at[d], dst_ref=recv_b.at[me], send_sem=s_bs,
                    recv_sem=s_br.at[l], device_id=(w2, l2), device_id_type=MESH,
                ).start()

            return c

        lax.fori_loop(0, 32, send_back, 0)
        return c

    for half in range(2):
        lax.fori_loop(4 * half, 4 * half + 4, arrive, 0)
        legendre_step(half)
        lax.fori_loop(4 * half, 4 * half + 4, send_group, 0)
    recv_b[me] = send_b[me]

    def returned(q, c):
        for u in range(2):
            src = lev_from(l, 7 - 2 * q - u)

            def landed(count, src=src):
                pltpu.make_async_remote_copy(
                    src_ref=send_b.at[pl.ds(0, count)], dst_ref=recv_b.at[pl.ds(0, count)],
                    send_sem=s_bs, recv_sem=s_br.at[src], device_id=(w, l), device_id_type=MESH,
                ).wait_recv()

            @pl.when(src == l)
            def _():
                landed(NWAVE - 1)

            @pl.when(src != l)
            def _():
                landed(NWAVE)

            for v in range(NWAVE):
                both = recv_b[v * NLEV + src].astype(F32)
                rows[64 * u + 2 * v] = both[0:8]
                rows[64 * u + 2 * v + 1] = both[8:16]
        lanes = pl.multiple_of(q * 128, 128)
        for j in range(8):
            turned[j, :, pl.ds(lanes, 128)] = rows[:, j, :].T.astype(BF16)
        return c

    lax.fori_loop(0, 4, returned, 0)

    for h in range(2):
        for p in range(2):
            for r in range(2):
                x = lax.dot_general(
                    turned[4 * h + 2 * p + r], onehot[...], NN, preferred_element_type=F32
                )
                limit = jnp.concatenate([column[h]] * 4, axis=1)
                twice = twice_wave(p, lane_iota((128, PAIRS)))
                x = jnp.where(twice.astype(F32) < limit, x, 0.0)
                x = x * (jnp.where(twice == 0, 1.0, 2.0) if p == 0 else 2.0)
                back[p, h * 128:(h + 1) * 128, r * PAIRS:(r + 1) * PAIRS] = x.astype(BF16)

    def write(x, start, width):
        for h in range(2):
            for f in range(4):
                row = h * 128 + f * 32
                grid[f, h, :, start:start + width] = x[row:row + 32].astype(BF16)

    tail = None
    before = None
    for start, width in BLOCKS:
        x = jnp.dot(back[0], table[0, :, start:start + width], preferred_element_type=F32)
        y = jnp.dot(back[1], table[1, :, start:start + width], preferred_element_type=F32)
        total = x + y
        differ = pltpu.roll(x - y, 64, 1)
        if width == 128:
            tail = differ
            before = total
        else:
            low = lane_iota((256, 128)) < 64
            write(total, start, 256)
            edge = jnp.where(low, before, differ[:, :128])
            write(jnp.concatenate([edge, differ[:, 128:]], axis=1), 2048 + start, 256)
            before = differ[:, :128]
    write(jnp.where(lane_iota((256, 128)) < 64, before, tail), 4096, 128)

    pltpu.make_async_remote_copy(
        src_ref=send_f.at[pl.ds(0, 255)], dst_ref=recv_f.at[pl.ds(0, 255)], send_sem=s_fs,
        recv_sem=s_g1r, device_id=(w, l), device_id_type=MESH,
    ).wait_send()
    pltpu.make_async_remote_copy(
        src_ref=send_b.at[pl.ds(0, 255)], dst_ref=recv_b.at[pl.ds(0, 255)], send_sem=s_bs,
        recv_sem=s_g1r, device_id=(w, l), device_id_type=MESH,
    ).wait_send()


def shards(grid_field, legendre, wave_groups, lat_weights, cycle_points, diffusion):
    dma = pltpu.SemaphoreType.DMA
    vmem = pl.BlockSpec(memory_space=pltpu.VMEM)
    hbm = pl.BlockSpec(memory_space=pltpu.HBM)
    table = jnp.asarray(basis_tables())
    by_row = legendre.reshape(2, ROWS, 8, 128).transpose(1, 2, 0, 3)
    return pl.pallas_call(
        exchange,
        out_shape=(
            pltpu.VMEM((2, 32, 2, ROWS), F32),
            pltpu.VMEM((4, 2, 32, NLON), BF16),
        ),
        in_specs=[hbm] * 7,
        out_specs=(vmem, vmem),
        scratch_shapes=[
            pltpu.VMEM((4, 2, 32, NLON), BF16),
            pltpu.VMEM((ROWS, 8, 2, 128), BF16),
            pltpu.VMEM((2, 1024, 1024), BF16),
            pltpu.VMEM((2, 16, 1024), BF16),
            pltpu.VMEM((2, 1024, WIDE), BF16),
            pltpu.VMEM((2, 256, WIDE), BF16),
            pltpu.VMEM((PAIRS, 8, 128), F32),
            pltpu.VMEM((256, 16, 128), BF16),
            pltpu.VMEM((256, 16, 128), BF16),
            pltpu.VMEM((2, 256, 1024), BF16),
            pltpu.VMEM((2, 256, ROWP), F32),
            pltpu.VMEM((2, 256, ROWP), BF16),
            pltpu.VMEM((2, 32, 8, 1024), F32),
            pltpu.VMEM((256, 16, 128), BF16),
            pltpu.VMEM((256, 16, 128), BF16),
            pltpu.VMEM((128, 8, 128), F32),
            pltpu.VMEM((8, 128, PAIRS), BF16),
            pltpu.VMEM((PAIRS, PAIRS), BF16),
            pltpu.VMEM((2, 128, 128), F32),
            pltpu.VMEM((2, 256, 1024), BF16),
            pltpu.VMEM((NLEV, 1, 128), jnp.int32),
            pltpu.VMEM((NWAVE, 1, 128), jnp.int32),
            pltpu.VMEM((4, 128), jnp.int32),
            pltpu.SMEM((4, 128), jnp.int32),
            pltpu.SMEM((2,), jnp.int32),
            pltpu.VMEM((1, 1024), F32),
            pltpu.VMEM((2, 1024), jnp.int32),
            pltpu.SMEM((32,), F32),
            dma((2,)), dma, dma, dma, dma((4,)), dma, dma, dma, dma, dma, dma((NLEV,)), dma,
            dma((NLEV,)),
        ],
        compiler_params=pltpu.CompilerParams(
            collective_id=0, has_side_effects=True, vmem_limit_bytes=56 << 20
        ),
        name="exchange",
    )(grid_field, by_row, table, wave_groups, lat_weights.reshape(1, -1), cycle_points, diffusion)


def solution(mesh):
    return jax.shard_map(
        shards,
        mesh=mesh,
        in_specs=(
            P("lev", None, "wave", None),
            P(("wave", "lev"), None, None),
            P(("wave", "lev")),
            P(),
            P(),
            P(),
        ),
        out_specs=(P(("wave", "lev"), None, None, None), P("lev", None, "wave", None)),
        check_vma=False,
    )
```

```python
import math

import jax
import jax.numpy as jnp
import ml_dtypes
import numpy as np
from jax import lax
from jax.experimental import pallas as pl
from jax.experimental.pallas import tpu as pltpu
from jax.sharding import PartitionSpec as P

WAVES = 1024
PAIRS = 512
NLON = 4224
HALF = NLON // 2
WIDE = 2176
ROWS = 1025
ROWP = 1152
NWAVE = 32
NLEV = 8
MESH = pl.DeviceIdType.MESH
F32 = jnp.float32
BF16 = jnp.bfloat16
NT = (((1,), (1,)), ((), ()))
NN = (((1,), (0,)), ((), ()))


def basis_tables():
    pairs = np.arange(PAIRS, dtype=np.int64)
    points = np.arange(HALF, dtype=np.int64)
    tables = np.zeros((2, 2, PAIRS, WIDE), np.float32)
    for p, waves in enumerate((2 * pairs, WAVES - 1 - 2 * pairs)):
        angles = (waves[:, None] * points[None, :] % NLON) * (2.0 * math.pi / NLON)
        tables[p, 0, :, :HALF] = np.cos(angles) / math.sqrt(NLON)
        tables[p, 1, :, :HALF] = -np.sin(angles) / math.sqrt(NLON)
    return tables.reshape(2, 2 * PAIRS, WIDE).astype(ml_dtypes.bfloat16)


def select8(index, values):
    result = jnp.int32(values[0])
    for k in range(1, len(values)):
        result = jnp.where(index == k, values[k], result)
    return result


Z_ORDER = (0, 1, 7, 2, 6, 3, 5, 4)
Y_ORDER = (0, 1, 3, 2)


def lev_offset(index):
    return select8(index % 4, Y_ORDER), index // 4


def lev_at(l, index):
    dx, dc = lev_offset(index)
    return (l // 2 + dx) % 4 * 2 + (l % 2 + dc) % 2


def lev_from(l, index):
    dx, dc = lev_offset(index)
    return (l // 2 + 4 - dx) % 4 * 2 + (l % 2 + dc) % 2


def target(w, l, dc, m):
    z = m % 8
    k = m // 8
    dz = select8(z, Z_ORDER)
    dx = select8((k + z) % 4, Y_ORDER)
    dy = select8((k // 4 + z // 2) % 4, Y_ORDER)
    w2 = (w // 4 + dz) % 8 * 4 + (w % 4 + dy) % 4
    return w2, (l // 2 + dx) % 4 * 2 + (l % 2 + dc) % 2


def sub_iota(shape):
    return lax.broadcasted_iota(jnp.int32, shape, len(shape) - 2)


def lane_iota(shape):
    return lax.broadcasted_iota(jnp.int32, shape, len(shape) - 1)


def swap_lane(a0, a1, a2, a3):
    lane = lane_iota(a0.shape)
    low64 = lane < 64
    low32 = lane % 64 < 32

    def roll(x, s):
        return pltpu.roll(x, s, 1)

    lo0 = jnp.where(low64, a0, roll(a2, 64))
    lo1 = jnp.where(low64, a1, roll(a3, 64))
    hi0 = jnp.where(low64, roll(a0, 64), a2)
    hi1 = jnp.where(low64, roll(a1, 64), a3)
    return (
        jnp.where(low32, lo0, roll(lo1, 32)),
        jnp.where(low32, roll(lo0, 96), lo1),
        jnp.where(low32, hi0, roll(hi1, 32)),
        jnp.where(low32, roll(hi0, 96), hi1),
    )


BLOCKS = [(2048, 128)] + [(256 * n, 256) for n in range(8)]


def exchange(
    field_hbm, leg_hbm, table_hbm, ids_hbm, weights_hbm, points_hbm, diffusion_hbm,
    spec, grid,
    field, raw, leg, last, table, fold, pairs, send_f, recv_f, oper, damp, dope, modes, send_b,
    recv_b, rows, turned, onehot, column, back, gat1, gat2, gatv, gats, ids, weights, points,
    diffusion,
    s_table, s_field, s_leg, s_local, s_small, s_g1s, s_g1r, s_g2s, s_g2r, s_fs, s_fr, s_bs, s_br,
):
    w = lax.axis_index("wave")
    l = lax.axis_index("lev")
    me = w * NLEV + l

    small_copies = [
        pltpu.make_async_copy(a, b, s_small.at[i])
        for i, (a, b) in enumerate((
            (ids_hbm, ids), (weights_hbm, weights), (points_hbm, points), (diffusion_hbm, diffusion),
        ))
    ]
    for copy in small_copies:
        copy.start()
    field_copy = pltpu.make_async_copy(field_hbm, field, s_field)
    field_copy.start()
    table_copies = [
        pltpu.make_async_copy(table_hbm.at[p], table.at[p], s_table.at[p]) for p in range(2)
    ]
    leg_copy = pltpu.make_async_copy(leg_hbm, raw, s_leg)

    barrier = pltpu.get_barrier_semaphore()

    def greet_lev(i, c):
        pl.semaphore_signal(barrier, inc=1, device_id=(w, (l + i) % NLEV), device_id_type=MESH)
        return c

    def greet_wave(i, c):
        pl.semaphore_signal(barrier, inc=1, device_id=((w + i) % NWAVE, l), device_id_type=MESH)
        return c

    lax.fori_loop(1, NLEV, greet_lev, 0)
    lax.fori_loop(1, NWAVE, greet_wave, 0)
    table_copies[0].start()

    for copy in small_copies:
        copy.wait()
    a0 = ids[0]
    a1 = ids[1]
    t0 = jnp.where(a0 % 2 == 0, a0 // 2, (WAVES - 1 - a0) // 2)
    t1 = jnp.where(a1 % 2 == 0, a1 // 2, (WAVES - 1 - a1) // 2)
    lane = lane_iota((1, 128))
    place = 2 * me % 128
    gat1[l] = jnp.where(lane == place, t0, 0) + jnp.where(lane == place + 1, t1, 0)

    band = pl.multiple_of(w // 4 * 128, 128)
    turn = (4 - w % 4) % 4 * 32
    lane1 = lane_iota((8, 128))

    def spread(row):
        moved = pltpu.roll(jnp.broadcast_to(row, (8, 128)), turn, 1)
        first = jnp.where(lane1 < 32, moved, jnp.zeros_like(moved))
        twice = first + pltpu.roll(first, 32, 1)
        return twice + pltpu.roll(twice, 64, 1)

    band_weights = spread(weights[:, pl.ds(band, 128)])
    band_points = [spread(points[h:h + 1, pl.ds(band, 128)]) for h in range(2)]

    pl.semaphore_wait(barrier, NLEV - 1 + NWAVE - 1)

    def send_g1(i, c):
        pltpu.make_async_remote_copy(
            src_ref=gat1.at[l], dst_ref=gat1.at[l], send_sem=s_g1s, recv_sem=s_g1r,
            device_id=(w, (l + i) % NLEV), device_id_type=MESH,
        ).start()
        return c

    lax.fori_loop(1, NLEV, send_g1, 0)

    field_copy.wait()
    table_copies[1].start()

    def fold_body(i, c):
        f = i // 4
        h = i // 2 % 2
        j = pl.multiple_of(i % 2 * 16, 16)
        first = field[f, h, pl.ds(j, 16), 0:WIDE].astype(F32)
        second = field[f, h, pl.ds(j, 16), NLON - WIDE:NLON].astype(F32)
        second = pltpu.roll(second, HALF, 1)
        row = pl.multiple_of(h * 128 + f * 32 + j, 16)
        fold[0, pl.ds(row, 16), :] = (first + second).astype(BF16)
        fold[1, pl.ds(row, 16), :] = (first - second).astype(BF16)
        return c

    lax.fori_loop(0, 16, fold_body, 0)

    g1 = pltpu.make_async_remote_copy(
        src_ref=gat1.at[pl.ds(0, NLEV - 1)], dst_ref=gat1.at[pl.ds(0, NLEV - 1)], send_sem=s_g1s,
        recv_sem=s_g1r, device_id=(w, l), device_id_type=MESH,
    )
    g1.wait_send()
    g1.wait_recv()
    total = gat1[0]
    for i in range(1, NLEV):
        total = total + gat1[i]
    gat2[w] = total

    def send_g2(i, c):
        pltpu.make_async_remote_copy(
            src_ref=gat2.at[w], dst_ref=gat2.at[w], send_sem=s_g2s, recv_sem=s_g2r,
            device_id=((w + i) % NWAVE, l), device_id_type=MESH,
        ).start()
        return c

    lax.fori_loop(1, NWAVE, send_g2, 0)

    def twice_wave(p, pair):
        return 4 * pair if p == 0 else 2 * (WAVES - 1) - 4 * pair

    def transform(p):
        def body(part, c):
            start = pl.multiple_of(part * PAIRS, PAIRS)
            out = lax.dot_general(
                table[p, pl.ds(start, PAIRS), :], fold[p], NT, preferred_element_type=F32
            )
            twice = twice_wave(p, sub_iota((PAIRS, 128)))
            north = jnp.where(twice < band_points[0][0:1, :], out[:, :128], 0.0)
            south = jnp.where(twice < band_points[1][0:1, :], out[:, 128:], 0.0)
            scale = band_weights[0:1, :]
            pairs[:, 2 * p + part, :] = (north + south) * scale
            pairs[:, 4 + 2 * p + part, :] = (north - south) * scale
            return c

        lax.fori_loop(0, 2, body, 0, unroll=2)

    table_copies[0].wait()
    transform(0)
    table_copies[1].wait()
    leg_copy.start()
    transform(1)

    g2 = pltpu.make_async_remote_copy(
        src_ref=gat2.at[pl.ds(0, NWAVE - 1)], dst_ref=gat2.at[pl.ds(0, NWAVE - 1)], send_sem=s_g2s,
        recv_sem=s_g2r, device_id=(w, l), device_id_type=MESH,
    )
    g2.wait_send()
    g2.wait_recv()
    for r in range(4):
        total = gat2[8 * r]
        for i in range(1, 8):
            total = total + gat2[8 * r + i]
        gatv[r:r + 1, :] = jnp.clip(total, 0, PAIRS - 1)
    ids_copy = pltpu.make_async_copy(gatv, gats, s_local)
    ids_copy.start()
    ids_copy.wait()

    def packed(d):
        first = gats[d // 64, 2 * d % 128]
        second = gats[d // 64, 2 * d % 128 + 1]
        return jnp.concatenate([pairs[first], pairs[second]], axis=0).astype(BF16)

    recv_f[me] = packed(me)

    def send_forward(i, c):
        j = 256 - i
        w2, l2 = target(w, l, j // 128, j % 128)
        d = w2 * NLEV + l2
        send_f[d] = packed(d)
        pltpu.make_async_remote_copy(
            src_ref=send_f.at[d], dst_ref=recv_f.at[me], send_sem=s_fs, recv_sem=s_fr.at[l],
            device_id=(w2, l2), device_id_type=MESH,
        ).start()
        return c

    lax.fori_loop(1, 256, send_forward, 0, unroll=5)

    leg_copy.wait()

    def relay(i, c):
        k = pl.multiple_of(i * 16, 16)
        for ch in range(8):
            x = raw[pl.ds(k, 16), ch].astype(F32)
            for s in range(2):
                leg[s, pl.ds(k, 16), ch * 128:(ch + 1) * 128] = x[:, s, :].astype(BF16)
        return c

    lax.fori_loop(0, 64, relay, 0)
    for ch in range(8):
        x = raw[1024, ch].astype(F32)
        for s in range(2):
            last[s, :, ch * 128:(ch + 1) * 128] = jnp.broadcast_to(x[s:s + 1], (16, 128)).astype(BF16)

    def field_of(g):
        core = (l + 1 + g // 16) % 2
        return (g // 4 % 4 * 2 + core) * 4 + g % 4

    def chosen(a, base, width):
        sub = sub_iota((8, width))
        k = base + lane_iota((8, width))
        is_a = k < WAVES - a
        parity = jnp.where(is_a, k % 2, (k + a) % 2)
        member = jnp.where(is_a, a % 2, 1 - a % 2)
        sel = (sub // 4 == parity) & (sub // 2 % 2 == member) & (k < ROWS)
        degree = jnp.where(is_a, a + k, k - 1)
        return sel, degree

    for s, a in enumerate((a0, a1)):
        sel, degree = chosen(a, 0, ROWP)
        level = degree.astype(F32)
        scaled = level * (level + 1.0) / (WAVES * (WAVES - 1.0))
        squared = scaled * scaled
        one = jnp.where(sel, 1.0, 0.0)

        def damp_body(f, c, s=s, squared=squared, one=one):
            row = pl.multiple_of(f * 8, 8)
            damp[s, pl.ds(row, 8), :] = one / (1.0 + diffusion[field_of(f)] * squared)
            return c

        lax.fori_loop(0, 32, damp_body, 0)

    def arrive(i, c):
        src = lev_from(l, 7 - i)

        def landed(count):
            pltpu.make_async_remote_copy(
                src_ref=send_f.at[pl.ds(0, count)], dst_ref=recv_f.at[pl.ds(0, count)],
                send_sem=s_fs, recv_sem=s_fr.at[src], device_id=(w, l), device_id_type=MESH,
            ).wait_recv()

        @pl.when(src == l)
        def _():
            landed(NWAVE - 1)

        @pl.when(src != l)
        def _():
            landed(NWAVE)

        for block in range(8):
            tiles = [recv_f[(4 * block + v) * NLEV + src].astype(F32) for v in range(4)]
            by_field = swap_lane(*tiles)
            for s in range(2):
                for pair in range(2):
                    row = pl.multiple_of(i // 4 * 128 + src // 2 * 32 + pair * 16, 16)
                    oper[s, pl.ds(row, 16), block * 128:(block + 1) * 128] = jnp.concatenate(
                        [
                            by_field[2 * pair][8 * s:8 * s + 8],
                            by_field[2 * pair + 1][8 * s:8 * s + 8],
                        ],
                        axis=0,
                    ).astype(BF16)
        return c

    def pick(half, s, a, x, start, width):
        sel, _ = chosen(a, start, width)
        lanes = pl.ds(start, width)
        for i in range(8):
            damped = []
            for g in (2 * i, 2 * i + 1):
                y = jnp.where(sel, x[8 * g:8 * g + 8], 0.0)
                y = y + pltpu.roll(y, 4, 0)
                y = y + pltpu.roll(y, 2, 0)
                f = field_of(16 * half + g)
                if width == 128:
                    spec[s, f, :, 1024:ROWS] = y[0:2, 0:1]
                else:
                    spec[s, f, :, lanes] = y[0:2]
                row = 128 * half + 8 * g
                damped.append(y * damp[s, row:row + 8, lanes])
            row = 128 * half + 16 * i
            dope[s, row:row + 16, lanes] = jnp.concatenate(damped, axis=0).astype(BF16)

    def legendre_step(half):
        mine = slice(128 * half, 128 * half + 128)

        def product(n, c):
            start = pl.multiple_of(n * 256, 256)
            for s, a in enumerate((a0, a1)):
                x = lax.dot_general(
                    oper[s, mine], leg[s, pl.ds(start, 256), :], NT, preferred_element_type=F32
                )
                pick(half, s, a, x, start, 256)
            return c

        lax.fori_loop(0, 4, product, 0, unroll=2)
        for s, a in enumerate((a0, a1)):
            rhs = jnp.concatenate([last[s]] * 8, axis=0)
            x = lax.dot_general(oper[s, mine], rhs, NT, preferred_element_type=F32)
            pick(half, s, a, x, 1024, 128)

        def inverse(n, c):
            start = pl.multiple_of(n * 256, 256)
            sign = jnp.where(sub_iota((1, 8, 256)) < 4, 1.0, -1.0)
            for s in range(2):
                x = lax.dot_general(
                    dope[s, mine, 0:1024], leg[s, 0:1024, pl.ds(start, 256)], NN,
                    preferred_element_type=F32,
                )
                edge = dope[s, mine, 1024:ROWP].astype(F32)[:, 0:1]
                x = x + edge * last[s, :, pl.ds(start, 256)].astype(F32)[0:1]
                x = x.reshape(16, 8, 256)
                modes[s, 16 * half:16 * half + 16, :, pl.ds(start, 256)] = (
                    x * sign + pltpu.roll(x, 4, 1)
                )
            return c

        lax.fori_loop(0, 4, inverse, 0, unroll=2)

    def send_group(i, c):
        l2 = lev_at(l, 7 - i)
        for block in range(8):
            lanes = slice(block * 128, (block + 1) * 128)
            tiles = [
                jnp.concatenate([modes[s, i // 4 * 16 + l2 // 2 * 4 + f, :, lanes] for s in range(2)], axis=0)
                for f in range(4)
            ]
            for u, x in enumerate(swap_lane(*tiles)):
                send_b[(4 * block + u) * NLEV + l2] = x.astype(BF16)
        return c

    for half in range(2):
        lax.fori_loop(4 * half, 4 * half + 4, arrive, 0)
        legendre_step(half)
        lax.fori_loop(4 * half, 4 * half + 4, send_group, 0)

        def send_back(m, c, half=half):
            w2, l2 = target(w, l, 1 - half, 127 - m)
            d = w2 * NLEV + l2

            @pl.when(d != me)
            def _():
                pltpu.make_async_remote_copy(
                    src_ref=send_b.at[d], dst_ref=recv_b.at[me], send_sem=s_bs,
                    recv_sem=s_br.at[l], device_id=(w2, l2), device_id_type=MESH,
                ).start()

            return c

        lax.fori_loop(0, 128, send_back, 0)
    recv_b[me] = send_b[me]

    holders = [jnp.zeros((1, 128), F32)] * 4
    for r in range(4):
        held = jnp.broadcast_to(gatv[r:r + 1, :].astype(F32), (128, 128)).T
        slot = (128 * r + sub_iota((128, 128))).astype(F32)
        for b in range(4):
            pair = (128 * b + lane_iota((128, 128))).astype(F32)
            hit = jnp.where(held == pair, slot, 0.0)
            holders[b] = holders[b] + jnp.sum(hit, axis=0, keepdims=True)
    holders = [holder.astype(jnp.int32) for holder in holders]

    for q in range(4):
        bases = [2 * lev_from(l, 7 - 2 * q - u) for u in range(2)]

        def onehot_body(b, c, q=q, bases=bases):
            sub = sub_iota((128, 128))
            slot = jnp.where(sub < 64, bases[0], bases[1]) + sub % 64 // 2 * 16 + sub % 2
            for b in range(4):
                hit = slot == holders[b]
                onehot[q * 128:(q + 1) * 128, b * 128:(b + 1) * 128] = jnp.where(
                    hit, 1.0, 0.0
                ).astype(BF16)
            return c

        lax.fori_loop(0, 1, onehot_body, 0)
    for h in range(2):
        column[h] = jnp.broadcast_to(band_points[h][0:1, :].astype(F32), (128, 128)).T

    def returned(q, c):
        for u in range(2):
            src = lev_from(l, 7 - 2 * q - u)

            def landed(count, src=src):
                pltpu.make_async_remote_copy(
                    src_ref=send_b.at[pl.ds(0, count)], dst_ref=recv_b.at[pl.ds(0, count)],
                    send_sem=s_bs, recv_sem=s_br.at[src], device_id=(w, l), device_id_type=MESH,
                ).wait_recv()

            @pl.when(src == l)
            def _():
                landed(NWAVE - 1)

            @pl.when(src != l)
            def _():
                landed(NWAVE)

            for v in range(NWAVE):
                both = recv_b[v * NLEV + src].astype(F32)
                rows[64 * u + 2 * v] = both[0:8]
                rows[64 * u + 2 * v + 1] = both[8:16]
        lanes = pl.multiple_of(q * 128, 128)
        for j in range(8):
            turned[j, :, pl.ds(lanes, 128)] = rows[:, j, :].T.astype(BF16)
        return c

    lax.fori_loop(0, 4, returned, 0)

    for h in range(2):
        for p in range(2):
            for r in range(2):
                x = lax.dot_general(
                    turned[4 * h + 2 * p + r], onehot[...], NN, preferred_element_type=F32
                )
                limit = jnp.concatenate([column[h]] * 4, axis=1)
                twice = twice_wave(p, lane_iota((128, PAIRS)))
                x = jnp.where(twice.astype(F32) < limit, x, 0.0)
                x = x * (jnp.where(twice == 0, 1.0, 2.0) if p == 0 else 2.0)
                back[p, h * 128:(h + 1) * 128, r * PAIRS:(r + 1) * PAIRS] = x.astype(BF16)

    def write(x, start, width):
        for h in range(2):
            for f in range(4):
                row = h * 128 + f * 32
                grid[f, h, :, start:start + width] = x[row:row + 32].astype(BF16)

    tail = None
    before = None
    for start, width in BLOCKS:
        x = jnp.dot(back[0], table[0, :, start:start + width], preferred_element_type=F32)
        y = jnp.dot(back[1], table[1, :, start:start + width], preferred_element_type=F32)
        total = x + y
        differ = pltpu.roll(x - y, 64, 1)
        if width == 128:
            tail = differ
            before = total
        else:
            low = lane_iota((256, 128)) < 64
            write(total, start, 256)
            edge = jnp.where(low, before, differ[:, :128])
            write(jnp.concatenate([edge, differ[:, 128:]], axis=1), 2048 + start, 256)
            before = differ[:, :128]
    write(jnp.where(lane_iota((256, 128)) < 64, before, tail), 4096, 128)

    pltpu.make_async_remote_copy(
        src_ref=send_f.at[pl.ds(0, 255)], dst_ref=recv_f.at[pl.ds(0, 255)], send_sem=s_fs,
        recv_sem=s_g1r, device_id=(w, l), device_id_type=MESH,
    ).wait_send()
    pltpu.make_async_remote_copy(
        src_ref=send_b.at[pl.ds(0, 255)], dst_ref=recv_b.at[pl.ds(0, 255)], send_sem=s_bs,
        recv_sem=s_g1r, device_id=(w, l), device_id_type=MESH,
    ).wait_send()


def shards(grid_field, legendre, wave_groups, lat_weights, cycle_points, diffusion):
    dma = pltpu.SemaphoreType.DMA
    vmem = pl.BlockSpec(memory_space=pltpu.VMEM)
    hbm = pl.BlockSpec(memory_space=pltpu.HBM)
    table = jnp.asarray(basis_tables())
    by_row = legendre.reshape(2, ROWS, 8, 128).transpose(1, 2, 0, 3)
    return pl.pallas_call(
        exchange,
        out_shape=(
            pltpu.VMEM((2, 32, 2, ROWS), F32),
            pltpu.VMEM((4, 2, 32, NLON), BF16),
        ),
        in_specs=[hbm] * 7,
        out_specs=(vmem, vmem),
        scratch_shapes=[
            pltpu.VMEM((4, 2, 32, NLON), BF16),
            pltpu.VMEM((ROWS, 8, 2, 128), BF16),
            pltpu.VMEM((2, 1024, 1024), BF16),
            pltpu.VMEM((2, 16, 1024), BF16),
            pltpu.VMEM((2, 1024, WIDE), BF16),
            pltpu.VMEM((2, 256, WIDE), BF16),
            pltpu.VMEM((PAIRS, 8, 128), F32),
            pltpu.VMEM((256, 16, 128), BF16),
            pltpu.VMEM((256, 16, 128), BF16),
            pltpu.VMEM((2, 256, 1024), BF16),
            pltpu.VMEM((2, 256, ROWP), F32),
            pltpu.VMEM((2, 256, ROWP), BF16),
            pltpu.VMEM((2, 32, 8, 1024), F32),
            pltpu.VMEM((256, 16, 128), BF16),
            pltpu.VMEM((256, 16, 128), BF16),
            pltpu.VMEM((128, 8, 128), F32),
            pltpu.VMEM((8, 128, PAIRS), BF16),
            pltpu.VMEM((PAIRS, PAIRS), BF16),
            pltpu.VMEM((2, 128, 128), F32),
            pltpu.VMEM((2, 256, 1024), BF16),
            pltpu.VMEM((NLEV, 1, 128), jnp.int32),
            pltpu.VMEM((NWAVE, 1, 128), jnp.int32),
            pltpu.VMEM((4, 128), jnp.int32),
            pltpu.SMEM((4, 128), jnp.int32),
            pltpu.SMEM((2,), jnp.int32),
            pltpu.VMEM((1, 1024), F32),
            pltpu.VMEM((2, 1024), jnp.int32),
            pltpu.SMEM((32,), F32),
            dma((2,)), dma, dma, dma, dma((4,)), dma, dma, dma, dma, dma, dma((NLEV,)), dma,
            dma((NLEV,)),
        ],
        compiler_params=pltpu.CompilerParams(
            collective_id=0, has_side_effects=True, vmem_limit_bytes=56 << 20
        ),
        name="exchange",
    )(grid_field, by_row, table, wave_groups, lat_weights.reshape(1, -1), cycle_points, diffusion)


def solution(mesh):
    return jax.shard_map(
        shards,
        mesh=mesh,
        in_specs=(
            P("lev", None, "wave", None),
            P(("wave", "lev"), None, None),
            P(("wave", "lev")),
            P(),
            P(),
            P(),
        ),
        out_specs=(P(("wave", "lev"), None, None, None), P("lev", None, "wave", None)),
        check_vma=False,
    )
```

```python
import math

import jax
import jax.numpy as jnp
import ml_dtypes
import numpy as np
from jax import lax
from jax.experimental import pallas as pl
from jax.experimental.pallas import tpu as pltpu
from jax.sharding import PartitionSpec as P

WAVES = 1024
PAIRS = 512
NLON = 4224
HALF = NLON // 2
WIDE = 2176
ROWS = 1025
ROWP = 1152
NWAVE = 32
NLEV = 8
MESH = pl.DeviceIdType.MESH
F32 = jnp.float32
BF16 = jnp.bfloat16
NT = (((1,), (1,)), ((), ()))
NN = (((1,), (0,)), ((), ()))


def basis_tables():
    pairs = np.arange(PAIRS, dtype=np.int64)
    points = np.arange(HALF, dtype=np.int64)
    tables = np.zeros((2, 2, PAIRS, WIDE), np.float32)
    for p, waves in enumerate((2 * pairs, WAVES - 1 - 2 * pairs)):
        angles = (waves[:, None] * points[None, :] % NLON) * (2.0 * math.pi / NLON)
        tables[p, 0, :, :HALF] = np.cos(angles) / math.sqrt(NLON)
        tables[p, 1, :, :HALF] = -np.sin(angles) / math.sqrt(NLON)
    return tables.reshape(2, 2 * PAIRS, WIDE).astype(ml_dtypes.bfloat16)


def select8(index, values):
    result = jnp.int32(values[0])
    for k in range(1, len(values)):
        result = jnp.where(index == k, values[k], result)
    return result


Z_ORDER = (0, 1, 7, 2, 6, 3, 5, 4)
Y_ORDER = (0, 1, 3, 2)


def lev_offset(index):
    return select8(index % 4, Y_ORDER), index // 4


def lev_at(l, index):
    dx, dc = lev_offset(index)
    return (l // 2 + dx) % 4 * 2 + (l % 2 + dc) % 2


def lev_from(l, index):
    dx, dc = lev_offset(index)
    return (l // 2 + 4 - dx) % 4 * 2 + (l % 2 + dc) % 2


def wave_at(w, index):
    dz = select8(index % 8, Z_ORDER)
    dy = select8(index // 8, Y_ORDER)
    return (w // 4 + dz) % 8 * 4 + (w % 4 + dy) % 4


def sub_iota(shape):
    return lax.broadcasted_iota(jnp.int32, shape, len(shape) - 2)


def lane_iota(shape):
    return lax.broadcasted_iota(jnp.int32, shape, len(shape) - 1)


def swap_lane(a0, a1, a2, a3):
    lane = lane_iota(a0.shape)
    low64 = lane < 64
    low32 = lane % 64 < 32

    def roll(x, s):
        return pltpu.roll(x, s, 1)

    lo0 = jnp.where(low64, a0, roll(a2, 64))
    lo1 = jnp.where(low64, a1, roll(a3, 64))
    hi0 = jnp.where(low64, roll(a0, 64), a2)
    hi1 = jnp.where(low64, roll(a1, 64), a3)
    return (
        jnp.where(low32, lo0, roll(lo1, 32)),
        jnp.where(low32, roll(lo0, 96), lo1),
        jnp.where(low32, hi0, roll(hi1, 32)),
        jnp.where(low32, roll(hi0, 96), hi1),
    )


BLOCKS = [(2048, 128)] + [(256 * n, 256) for n in range(8)]


def exchange(
    field_hbm, leg_hbm, table_hbm, ids_hbm, weights_hbm, points_hbm, diffusion_hbm,
    spec, grid,
    field, raw, leg, last, table, fold, pairs, send_f, recv_f, oper, damp, dope, modes, send_b,
    recv_b, rows, turned, onehot, column, back, gat1, gat2, gatv, gats, ids, weights, points,
    diffusion,
    s_table, s_field, s_leg, s_local, s_small, s_g1s, s_g1r, s_g2s, s_g2r, s_fs, s_fr, s_bs, s_br,
):
    w = lax.axis_index("wave")
    l = lax.axis_index("lev")
    me = w * NLEV + l

    small_copies = [
        pltpu.make_async_copy(a, b, s_small.at[i])
        for i, (a, b) in enumerate((
            (ids_hbm, ids), (weights_hbm, weights), (points_hbm, points), (diffusion_hbm, diffusion),
        ))
    ]
    for copy in small_copies:
        copy.start()
    field_copy = pltpu.make_async_copy(field_hbm, field, s_field)
    field_copy.start()
    table_copies = [
        pltpu.make_async_copy(table_hbm.at[p], table.at[p], s_table.at[p]) for p in range(2)
    ]
    leg_copy = pltpu.make_async_copy(leg_hbm, raw, s_leg)

    barrier = pltpu.get_barrier_semaphore()

    def greet_lev(i, c):
        pl.semaphore_signal(barrier, inc=1, device_id=(w, (l + i) % NLEV), device_id_type=MESH)
        return c

    def greet_wave(i, c):
        pl.semaphore_signal(barrier, inc=1, device_id=((w + i) % NWAVE, l), device_id_type=MESH)
        return c

    lax.fori_loop(1, NLEV, greet_lev, 0)
    lax.fori_loop(1, NWAVE, greet_wave, 0)
    table_copies[0].start()

    for copy in small_copies:
        copy.wait()
    a0 = ids[0]
    a1 = ids[1]
    t0 = jnp.where(a0 % 2 == 0, a0 // 2, (WAVES - 1 - a0) // 2)
    t1 = jnp.where(a1 % 2 == 0, a1 // 2, (WAVES - 1 - a1) // 2)
    lane = lane_iota((1, 128))
    place = 2 * me % 128
    gat1[l] = jnp.where(lane == place, t0, 0) + jnp.where(lane == place + 1, t1, 0)

    band = pl.multiple_of(w // 4 * 128, 128)
    turn = (4 - w % 4) % 4 * 32
    lane1 = lane_iota((8, 128))

    def spread(row):
        moved = pltpu.roll(jnp.broadcast_to(row, (8, 128)), turn, 1)
        first = jnp.where(lane1 < 32, moved, jnp.zeros_like(moved))
        twice = first + pltpu.roll(first, 32, 1)
        return twice + pltpu.roll(twice, 64, 1)

    band_weights = spread(weights[:, pl.ds(band, 128)])
    band_points = [spread(points[h:h + 1, pl.ds(band, 128)]) for h in range(2)]

    pl.semaphore_wait(barrier, NLEV - 1 + NWAVE - 1)

    def send_g1(i, c):
        pltpu.make_async_remote_copy(
            src_ref=gat1.at[l], dst_ref=gat1.at[l], send_sem=s_g1s, recv_sem=s_g1r,
            device_id=(w, (l + i) % NLEV), device_id_type=MESH,
        ).start()
        return c

    lax.fori_loop(1, NLEV, send_g1, 0)

    field_copy.wait()
    table_copies[1].start()

    def fold_body(i, c):
        f = i // 4
        h = i // 2 % 2
        j = pl.multiple_of(i % 2 * 16, 16)
        first = field[f, h, pl.ds(j, 16), 0:WIDE].astype(F32)
        second = field[f, h, pl.ds(j, 16), NLON - WIDE:NLON].astype(F32)
        second = pltpu.roll(second, HALF, 1)
        row = pl.multiple_of(h * 128 + f * 32 + j, 16)
        fold[0, pl.ds(row, 16), :] = (first + second).astype(BF16)
        fold[1, pl.ds(row, 16), :] = (first - second).astype(BF16)
        return c

    lax.fori_loop(0, 16, fold_body, 0)

    g1 = pltpu.make_async_remote_copy(
        src_ref=gat1.at[pl.ds(0, NLEV - 1)], dst_ref=gat1.at[pl.ds(0, NLEV - 1)], send_sem=s_g1s,
        recv_sem=s_g1r, device_id=(w, l), device_id_type=MESH,
    )
    g1.wait_send()
    g1.wait_recv()
    total = gat1[0]
    for i in range(1, NLEV):
        total = total + gat1[i]
    gat2[w] = total

    def send_g2(i, c):
        pltpu.make_async_remote_copy(
            src_ref=gat2.at[w], dst_ref=gat2.at[w], send_sem=s_g2s, recv_sem=s_g2r,
            device_id=((w + i) % NWAVE, l), device_id_type=MESH,
        ).start()
        return c

    lax.fori_loop(1, NWAVE, send_g2, 0)

    def twice_wave(p, pair):
        return 4 * pair if p == 0 else 2 * (WAVES - 1) - 4 * pair

    def transform(p):
        def body(part, c):
            start = pl.multiple_of(part * PAIRS, PAIRS)
            out = lax.dot_general(
                table[p, pl.ds(start, PAIRS), :], fold[p], NT, preferred_element_type=F32
            )
            twice = twice_wave(p, sub_iota((PAIRS, 128)))
            north = jnp.where(twice < band_points[0][0:1, :], out[:, :128], 0.0)
            south = jnp.where(twice < band_points[1][0:1, :], out[:, 128:], 0.0)
            scale = band_weights[0:1, :]
            pairs[:, 2 * p + part, :] = (north + south) * scale
            pairs[:, 4 + 2 * p + part, :] = (north - south) * scale
            return c

        lax.fori_loop(0, 2, body, 0, unroll=2)

    table_copies[0].wait()
    transform(0)
    table_copies[1].wait()
    leg_copy.start()
    transform(1)

    g2 = pltpu.make_async_remote_copy(
        src_ref=gat2.at[pl.ds(0, NWAVE - 1)], dst_ref=gat2.at[pl.ds(0, NWAVE - 1)], send_sem=s_g2s,
        recv_sem=s_g2r, device_id=(w, l), device_id_type=MESH,
    )
    g2.wait_send()
    g2.wait_recv()
    for r in range(4):
        total = gat2[8 * r]
        for i in range(1, 8):
            total = total + gat2[8 * r + i]
        gatv[r:r + 1, :] = jnp.clip(total, 0, PAIRS - 1)
    ids_copy = pltpu.make_async_copy(gatv, gats, s_local)
    ids_copy.start()
    ids_copy.wait()

    def packed(d):
        first = gats[d // 64, 2 * d % 128]
        second = gats[d // 64, 2 * d % 128 + 1]
        return jnp.concatenate([pairs[first], pairs[second]], axis=0).astype(BF16)

    recv_f[me] = packed(me)

    def send_forward(i, c):
        j = 256 - i
        w2 = wave_at(w, j % NWAVE)
        l2 = lev_at(l, j // NWAVE)
        d = w2 * NLEV + l2
        send_f[d] = packed(d)
        pltpu.make_async_remote_copy(
            src_ref=send_f.at[d], dst_ref=recv_f.at[me], send_sem=s_fs, recv_sem=s_fr.at[l],
            device_id=(w2, l2), device_id_type=MESH,
        ).start()
        return c

    lax.fori_loop(1, 256, send_forward, 0, unroll=5)

    leg_copy.wait()

    def relay(i, c):
        k = pl.multiple_of(i * 16, 16)
        for ch in range(8):
            x = raw[pl.ds(k, 16), ch].astype(F32)
            for s in range(2):
                leg[s, pl.ds(k, 16), ch * 128:(ch + 1) * 128] = x[:, s, :].astype(BF16)
        return c

    lax.fori_loop(0, 64, relay, 0)
    for ch in range(8):
        x = raw[1024, ch].astype(F32)
        for s in range(2):
            last[s, :, ch * 128:(ch + 1) * 128] = jnp.broadcast_to(x[s:s + 1], (16, 128)).astype(BF16)

    def field_of(g):
        core = (l + 1 + g // 16) % 2
        return (g // 4 % 4 * 2 + core) * 4 + g % 4

    def chosen(a, base, width):
        sub = sub_iota((8, width))
        k = base + lane_iota((8, width))
        is_a = k < WAVES - a
        parity = jnp.where(is_a, k % 2, (k + a) % 2)
        member = jnp.where(is_a, a % 2, 1 - a % 2)
        sel = (sub // 4 == parity) & (sub // 2 % 2 == member) & (k < ROWS)
        degree = jnp.where(is_a, a + k, k - 1)
        return sel, degree

    for s, a in enumerate((a0, a1)):
        sel, degree = chosen(a, 0, ROWP)
        level = degree.astype(F32)
        scaled = level * (level + 1.0) / (WAVES * (WAVES - 1.0))
        squared = scaled * scaled
        one = jnp.where(sel, 1.0, 0.0)

        def damp_body(f, c, s=s, squared=squared, one=one):
            row = pl.multiple_of(f * 8, 8)
            damp[s, pl.ds(row, 8), :] = one / (1.0 + diffusion[field_of(f)] * squared)
            return c

        lax.fori_loop(0, 32, damp_body, 0)

    def arrive(i, c):
        src = lev_from(l, 7 - i)

        def landed(count):
            pltpu.make_async_remote_copy(
                src_ref=send_f.at[pl.ds(0, count)], dst_ref=recv_f.at[pl.ds(0, count)],
                send_sem=s_fs, recv_sem=s_fr.at[src], device_id=(w, l), device_id_type=MESH,
            ).wait_recv()

        @pl.when(src == l)
        def _():
            landed(NWAVE - 1)

        @pl.when(src != l)
        def _():
            landed(NWAVE)

        for block in range(8):
            tiles = [recv_f[(4 * block + v) * NLEV + src].astype(F32) for v in range(4)]
            by_field = swap_lane(*tiles)
            for s in range(2):
                for pair in range(2):
                    row = pl.multiple_of(i // 4 * 128 + src // 2 * 32 + pair * 16, 16)
                    oper[s, pl.ds(row, 16), block * 128:(block + 1) * 128] = jnp.concatenate(
                        [
                            by_field[2 * pair][8 * s:8 * s + 8],
                            by_field[2 * pair + 1][8 * s:8 * s + 8],
                        ],
                        axis=0,
                    ).astype(BF16)
        return c

    def pick(half, s, a, x, start, width):
        sel, _ = chosen(a, start, width)
        lanes = pl.ds(start, width)
        for i in range(8):
            damped = []
            for g in (2 * i, 2 * i + 1):
                y = jnp.where(sel, x[8 * g:8 * g + 8], 0.0)
                y = y + pltpu.roll(y, 4, 0)
                y = y + pltpu.roll(y, 2, 0)
                f = field_of(16 * half + g)
                if width == 128:
                    spec[s, f, :, 1024:ROWS] = y[0:2, 0:1]
                else:
                    spec[s, f, :, lanes] = y[0:2]
                row = 128 * half + 8 * g
                damped.append(y * damp[s, row:row + 8, lanes])
            row = 128 * half + 16 * i
            dope[s, row:row + 16, lanes] = jnp.concatenate(damped, axis=0).astype(BF16)

    def legendre_step(half):
        mine = slice(128 * half, 128 * half + 128)

        def product(n, c):
            start = pl.multiple_of(n * 256, 256)
            for s, a in enumerate((a0, a1)):
                x = lax.dot_general(
                    oper[s, mine], leg[s, pl.ds(start, 256), :], NT, preferred_element_type=F32
                )
                pick(half, s, a, x, start, 256)
            return c

        lax.fori_loop(0, 4, product, 0, unroll=2)
        for s, a in enumerate((a0, a1)):
            rhs = jnp.concatenate([last[s]] * 8, axis=0)
            x = lax.dot_general(oper[s, mine], rhs, NT, preferred_element_type=F32)
            pick(half, s, a, x, 1024, 128)

        def inverse(n, c):
            start = pl.multiple_of(n * 256, 256)
            sign = jnp.where(sub_iota((1, 8, 256)) < 4, 1.0, -1.0)
            for s in range(2):
                x = lax.dot_general(
                    dope[s, mine, 0:1024], leg[s, 0:1024, pl.ds(start, 256)], NN,
                    preferred_element_type=F32,
                )
                edge = dope[s, mine, 1024:ROWP].astype(F32)[:, 0:1]
                x = x + edge * last[s, :, pl.ds(start, 256)].astype(F32)[0:1]
                x = x.reshape(16, 8, 256)
                modes[s, 16 * half:16 * half + 16, :, pl.ds(start, 256)] = (
                    x * sign + pltpu.roll(x, 4, 1)
                )
            return c

        lax.fori_loop(0, 4, inverse, 0, unroll=2)

    def send_group(i, c):
        l2 = lev_at(l, 7 - i)
        for block in range(8):
            lanes = slice(block * 128, (block + 1) * 128)
            tiles = [
                jnp.concatenate([modes[s, i // 4 * 16 + l2 // 2 * 4 + f, :, lanes] for s in range(2)], axis=0)
                for f in range(4)
            ]
            for u, x in enumerate(swap_lane(*tiles)):
                send_b[(4 * block + u) * NLEV + l2] = x.astype(BF16)

        def send_back(m, c):
            w2 = wave_at(w, 31 - m)
            d = w2 * NLEV + l2

            @pl.when(d != me)
            def _():
                pltpu.make_async_remote_copy(
                    src_ref=send_b.at[d], dst_ref=recv_b.at[me], send_sem=s_bs,
                    recv_sem=s_br.at[l], device_id=(w2, l2), device_id_type=MESH,
                ).start()

            return c

        lax.fori_loop(0, 32, send_back, 0)
        return c

    for half in range(2):
        lax.fori_loop(4 * half, 4 * half + 4, arrive, 0)
        legendre_step(half)
        lax.fori_loop(4 * half, 4 * half + 4, send_group, 0)
    recv_b[me] = send_b[me]

    holders = [jnp.zeros((1, 128), F32)] * 4
    for r in range(4):
        held = jnp.broadcast_to(gatv[r:r + 1, :].astype(F32), (128, 128)).T
        slot = (128 * r + sub_iota((128, 128))).astype(F32)
        for b in range(4):
            pair = (128 * b + lane_iota((128, 128))).astype(F32)
            hit = jnp.where(held == pair, slot, 0.0)
            holders[b] = holders[b] + jnp.sum(hit, axis=0, keepdims=True)
    holders = [holder.astype(jnp.int32) for holder in holders]

    for q in range(4):
        bases = [2 * lev_from(l, 7 - 2 * q - u) for u in range(2)]

        def onehot_body(b, c, q=q, bases=bases):
            sub = sub_iota((128, 128))
            slot = jnp.where(sub < 64, bases[0], bases[1]) + sub % 64 // 2 * 16 + sub % 2
            for b in range(4):
                hit = slot == holders[b]
                onehot[q * 128:(q + 1) * 128, b * 128:(b + 1) * 128] = jnp.where(
                    hit, 1.0, 0.0
                ).astype(BF16)
            return c

        lax.fori_loop(0, 1, onehot_body, 0)
    for h in range(2):
        column[h] = jnp.broadcast_to(band_points[h][0:1, :].astype(F32), (128, 128)).T

    def returned(q, c):
        for u in range(2):
            src = lev_from(l, 7 - 2 * q - u)

            def landed(count, src=src):
                pltpu.make_async_remote_copy(
                    src_ref=send_b.at[pl.ds(0, count)], dst_ref=recv_b.at[pl.ds(0, count)],
                    send_sem=s_bs, recv_sem=s_br.at[src], device_id=(w, l), device_id_type=MESH,
                ).wait_recv()

            @pl.when(src == l)
            def _():
                landed(NWAVE - 1)

            @pl.when(src != l)
            def _():
                landed(NWAVE)

            for v in range(NWAVE):
                both = recv_b[v * NLEV + src].astype(F32)
                rows[64 * u + 2 * v] = both[0:8]
                rows[64 * u + 2 * v + 1] = both[8:16]
        lanes = pl.multiple_of(q * 128, 128)
        for j in range(8):
            turned[j, :, pl.ds(lanes, 128)] = rows[:, j, :].T.astype(BF16)
        return c

    lax.fori_loop(0, 4, returned, 0)

    for h in range(2):
        for p in range(2):
            for r in range(2):
                x = lax.dot_general(
                    turned[4 * h + 2 * p + r], onehot[...], NN, preferred_element_type=F32
                )
                limit = jnp.concatenate([column[h]] * 4, axis=1)
                twice = twice_wave(p, lane_iota((128, PAIRS)))
                x = jnp.where(twice.astype(F32) < limit, x, 0.0)
                x = x * (jnp.where(twice == 0, 1.0, 2.0) if p == 0 else 2.0)
                back[p, h * 128:(h + 1) * 128, r * PAIRS:(r + 1) * PAIRS] = x.astype(BF16)

    def write(x, start, width):
        for h in range(2):
            for f in range(4):
                row = h * 128 + f * 32
                grid[f, h, :, start:start + width] = x[row:row + 32].astype(BF16)

    tail = None
    before = None
    for start, width in BLOCKS:
        x = jnp.dot(back[0], table[0, :, start:start + width], preferred_element_type=F32)
        y = jnp.dot(back[1], table[1, :, start:start + width], preferred_element_type=F32)
        total = x + y
        differ = pltpu.roll(x - y, 64, 1)
        if width == 128:
            tail = differ
            before = total
        else:
            low = lane_iota((256, 128)) < 64
            write(total, start, 256)
            edge = jnp.where(low, before, differ[:, :128])
            write(jnp.concatenate([edge, differ[:, 128:]], axis=1), 2048 + start, 256)
            before = differ[:, :128]
    write(jnp.where(lane_iota((256, 128)) < 64, before, tail), 4096, 128)

    pltpu.make_async_remote_copy(
        src_ref=send_f.at[pl.ds(0, 255)], dst_ref=recv_f.at[pl.ds(0, 255)], send_sem=s_fs,
        recv_sem=s_g1r, device_id=(w, l), device_id_type=MESH,
    ).wait_send()
    pltpu.make_async_remote_copy(
        src_ref=send_b.at[pl.ds(0, 255)], dst_ref=recv_b.at[pl.ds(0, 255)], send_sem=s_bs,
        recv_sem=s_g1r, device_id=(w, l), device_id_type=MESH,
    ).wait_send()


def shards(grid_field, legendre, wave_groups, lat_weights, cycle_points, diffusion):
    dma = pltpu.SemaphoreType.DMA
    vmem = pl.BlockSpec(memory_space=pltpu.VMEM)
    hbm = pl.BlockSpec(memory_space=pltpu.HBM)
    table = jnp.asarray(basis_tables())
    by_row = legendre.reshape(2, ROWS, 8, 128).transpose(1, 2, 0, 3)
    return pl.pallas_call(
        exchange,
        out_shape=(
            pltpu.VMEM((2, 32, 2, ROWS), F32),
            pltpu.VMEM((4, 2, 32, NLON), BF16),
        ),
        in_specs=[hbm] * 7,
        out_specs=(vmem, vmem),
        scratch_shapes=[
            pltpu.VMEM((4, 2, 32, NLON), BF16),
            pltpu.VMEM((ROWS, 8, 2, 128), BF16),
            pltpu.VMEM((2, 1024, 1024), BF16),
            pltpu.VMEM((2, 16, 1024), BF16),
            pltpu.VMEM((2, 1024, WIDE), BF16),
            pltpu.VMEM((2, 256, WIDE), BF16),
            pltpu.VMEM((PAIRS, 8, 128), F32),
            pltpu.VMEM((256, 16, 128), BF16),
            pltpu.VMEM((256, 16, 128), BF16),
            pltpu.VMEM((2, 256, 1024), BF16),
            pltpu.VMEM((2, 256, ROWP), F32),
            pltpu.VMEM((2, 256, ROWP), BF16),
            pltpu.VMEM((2, 32, 8, 1024), F32),
            pltpu.VMEM((256, 16, 128), BF16),
            pltpu.VMEM((256, 16, 128), BF16),
            pltpu.VMEM((128, 8, 128), F32),
            pltpu.VMEM((8, 128, PAIRS), BF16),
            pltpu.VMEM((PAIRS, PAIRS), BF16),
            pltpu.VMEM((2, 128, 128), F32),
            pltpu.VMEM((2, 256, 1024), BF16),
            pltpu.VMEM((NLEV, 1, 128), jnp.int32),
            pltpu.VMEM((NWAVE, 1, 128), jnp.int32),
            pltpu.VMEM((4, 128), jnp.int32),
            pltpu.SMEM((4, 128), jnp.int32),
            pltpu.SMEM((2,), jnp.int32),
            pltpu.VMEM((1, 1024), F32),
            pltpu.VMEM((2, 1024), jnp.int32),
            pltpu.SMEM((32,), F32),
            dma((2,)), dma, dma, dma, dma((4,)), dma, dma, dma, dma, dma, dma((NLEV,)), dma,
            dma((NLEV,)),
        ],
        compiler_params=pltpu.CompilerParams(
            collective_id=0, has_side_effects=True, vmem_limit_bytes=56 << 20
        ),
        name="exchange",
    )(grid_field, by_row, table, wave_groups, lat_weights.reshape(1, -1), cycle_points, diffusion)


def solution(mesh):
    return jax.shard_map(
        shards,
        mesh=mesh,
        in_specs=(
            P("lev", None, "wave", None),
            P(("wave", "lev"), None, None),
            P(("wave", "lev")),
            P(),
            P(),
            P(),
        ),
        out_specs=(P(("wave", "lev"), None, None, None), P("lev", None, "wave", None)),
        check_vma=False,
    )
```

```python
import math

import jax
import jax.numpy as jnp
import ml_dtypes
import numpy as np
from jax import lax
from jax.experimental import pallas as pl
from jax.experimental.pallas import tpu as pltpu
from jax.sharding import PartitionSpec as P

WAVES = 1024
PAIRS = 512
NLON = 4224
HALF = NLON // 2
WIDE = 2176
ROWS = 1025
ROWP = 1152
NWAVE = 32
NLEV = 8
MESH = pl.DeviceIdType.MESH
F32 = jnp.float32
BF16 = jnp.bfloat16
NT = (((1,), (1,)), ((), ()))
NN = (((1,), (0,)), ((), ()))


def basis_tables():
    pairs = np.arange(PAIRS, dtype=np.int64)
    points = np.arange(HALF, dtype=np.int64)
    tables = np.zeros((2, 2, PAIRS, WIDE), np.float32)
    for p, waves in enumerate((2 * pairs, WAVES - 1 - 2 * pairs)):
        angles = (waves[:, None] * points[None, :] % NLON) * (2.0 * math.pi / NLON)
        tables[p, 0, :, :HALF] = np.cos(angles) / math.sqrt(NLON)
        tables[p, 1, :, :HALF] = -np.sin(angles) / math.sqrt(NLON)
    return tables.reshape(2, 2 * PAIRS, WIDE).astype(ml_dtypes.bfloat16)


def select8(index, values):
    result = jnp.int32(values[0])
    for k in range(1, len(values)):
        result = jnp.where(index == k, values[k], result)
    return result


Z_ORDER = (0, 1, 7, 2, 6, 3, 5, 4)
Y_ORDER = (0, 1, 3, 2)


def lev_offset(index):
    return select8(index % 4, Y_ORDER), index // 4


def lev_at(l, index):
    dx, dc = lev_offset(index)
    return (l // 2 + dx) % 4 * 2 + (l % 2 + dc) % 2


def lev_from(l, index):
    dx, dc = lev_offset(index)
    return (l // 2 + 4 - dx) % 4 * 2 + (l % 2 + dc) % 2


def wave_at(w, index):
    dz = select8(index % 8, Z_ORDER)
    dy = select8(index // 8, Y_ORDER)
    return (w // 4 + dz) % 8 * 4 + (w % 4 + dy) % 4


def sub_iota(shape):
    return lax.broadcasted_iota(jnp.int32, shape, len(shape) - 2)


def lane_iota(shape):
    return lax.broadcasted_iota(jnp.int32, shape, len(shape) - 1)


def swap_lane(a0, a1, a2, a3):
    lane = lane_iota(a0.shape)
    low64 = lane < 64
    low32 = lane % 64 < 32

    def roll(x, s):
        return pltpu.roll(x, s, 1)

    lo0 = jnp.where(low64, a0, roll(a2, 64))
    lo1 = jnp.where(low64, a1, roll(a3, 64))
    hi0 = jnp.where(low64, roll(a0, 64), a2)
    hi1 = jnp.where(low64, roll(a1, 64), a3)
    return (
        jnp.where(low32, lo0, roll(lo1, 32)),
        jnp.where(low32, roll(lo0, 96), lo1),
        jnp.where(low32, hi0, roll(hi1, 32)),
        jnp.where(low32, roll(hi0, 96), hi1),
    )


BLOCKS = [(2048, 128)] + [(256 * n, 256) for n in range(8)]


def exchange(
    field_hbm, leg_hbm, table_hbm, ids_hbm, weights_hbm, points_hbm, diffusion_hbm,
    spec, grid,
    field, raw, leg, last, table, fold, pairs, send_f, recv_f, oper, damp, dope, modes, send_b,
    recv_b, rows, turned, onehot, column, back, gat1, gat2, gatv, gats, ids, weights, points,
    diffusion,
    s_table, s_field, s_leg, s_local, s_small, s_g1s, s_g1r, s_g2s, s_g2r, s_fs, s_fr, s_bs, s_br,
):
    w = lax.axis_index("wave")
    l = lax.axis_index("lev")
    me = w * NLEV + l

    small_copies = [
        pltpu.make_async_copy(a, b, s_small.at[i])
        for i, (a, b) in enumerate((
            (ids_hbm, ids), (weights_hbm, weights), (points_hbm, points), (diffusion_hbm, diffusion),
        ))
    ]
    for copy in small_copies:
        copy.start()
    field_copy = pltpu.make_async_copy(field_hbm, field, s_field)
    field_copy.start()
    table_copies = [
        pltpu.make_async_copy(table_hbm.at[p], table.at[p], s_table.at[p]) for p in range(2)
    ]
    leg_copy = pltpu.make_async_copy(leg_hbm, raw, s_leg)

    barrier = pltpu.get_barrier_semaphore()

    def greet_lev(i, c):
        pl.semaphore_signal(barrier, inc=1, device_id=(w, (l + i) % NLEV), device_id_type=MESH)
        return c

    def greet_wave(i, c):
        pl.semaphore_signal(barrier, inc=1, device_id=((w + i) % NWAVE, l), device_id_type=MESH)
        return c

    lax.fori_loop(1, NLEV, greet_lev, 0)
    lax.fori_loop(1, NWAVE, greet_wave, 0)
    table_copies[0].start()

    for copy in small_copies:
        copy.wait()
    a0 = ids[0]
    a1 = ids[1]
    t0 = jnp.where(a0 % 2 == 0, a0 // 2, (WAVES - 1 - a0) // 2)
    t1 = jnp.where(a1 % 2 == 0, a1 // 2, (WAVES - 1 - a1) // 2)
    lane = lane_iota((1, 128))
    place = 2 * me % 128
    gat1[l] = jnp.where(lane == place, t0, 0) + jnp.where(lane == place + 1, t1, 0)

    band = pl.multiple_of(w // 4 * 128, 128)
    turn = (4 - w % 4) % 4 * 32
    lane1 = lane_iota((8, 128))

    def spread(row):
        moved = pltpu.roll(jnp.broadcast_to(row, (8, 128)), turn, 1)
        first = jnp.where(lane1 < 32, moved, jnp.zeros_like(moved))
        twice = first + pltpu.roll(first, 32, 1)
        return twice + pltpu.roll(twice, 64, 1)

    band_weights = spread(weights[:, pl.ds(band, 128)])
    band_points = [spread(points[h:h + 1, pl.ds(band, 128)]) for h in range(2)]

    pl.semaphore_wait(barrier, NLEV - 1 + NWAVE - 1)

    def send_g1(i, c):
        pltpu.make_async_remote_copy(
            src_ref=gat1.at[l], dst_ref=gat1.at[l], send_sem=s_g1s, recv_sem=s_g1r,
            device_id=(w, (l + i) % NLEV), device_id_type=MESH,
        ).start()
        return c

    lax.fori_loop(1, NLEV, send_g1, 0)

    field_copy.wait()
    table_copies[1].start()

    def fold_body(i, c):
        f = i // 4
        h = i // 2 % 2
        j = pl.multiple_of(i % 2 * 16, 16)
        first = field[f, h, pl.ds(j, 16), 0:WIDE].astype(F32)
        second = field[f, h, pl.ds(j, 16), NLON - WIDE:NLON].astype(F32)
        second = pltpu.roll(second, HALF, 1)
        row = pl.multiple_of(h * 128 + f * 32 + j, 16)
        fold[0, pl.ds(row, 16), :] = (first + second).astype(BF16)
        fold[1, pl.ds(row, 16), :] = (first - second).astype(BF16)
        return c

    lax.fori_loop(0, 16, fold_body, 0)

    g1 = pltpu.make_async_remote_copy(
        src_ref=gat1.at[pl.ds(0, NLEV - 1)], dst_ref=gat1.at[pl.ds(0, NLEV - 1)], send_sem=s_g1s,
        recv_sem=s_g1r, device_id=(w, l), device_id_type=MESH,
    )
    g1.wait_send()
    g1.wait_recv()
    total = gat1[0]
    for i in range(1, NLEV):
        total = total + gat1[i]
    gat2[w] = total

    def send_g2(i, c):
        pltpu.make_async_remote_copy(
            src_ref=gat2.at[w], dst_ref=gat2.at[w], send_sem=s_g2s, recv_sem=s_g2r,
            device_id=((w + i) % NWAVE, l), device_id_type=MESH,
        ).start()
        return c

    lax.fori_loop(1, NWAVE, send_g2, 0)

    def twice_wave(p, pair):
        return 4 * pair if p == 0 else 2 * (WAVES - 1) - 4 * pair

    def transform(p):
        def body(part, c):
            start = pl.multiple_of(part * PAIRS, PAIRS)
            out = lax.dot_general(
                table[p, pl.ds(start, PAIRS), :], fold[p], NT, preferred_element_type=F32
            )
            twice = twice_wave(p, sub_iota((PAIRS, 128)))
            north = jnp.where(twice < band_points[0][0:1, :], out[:, :128], 0.0)
            south = jnp.where(twice < band_points[1][0:1, :], out[:, 128:], 0.0)
            scale = band_weights[0:1, :]
            pairs[:, 2 * p + part, :] = (north + south) * scale
            pairs[:, 4 + 2 * p + part, :] = (north - south) * scale
            return c

        lax.fori_loop(0, 2, body, 0, unroll=2)

    table_copies[0].wait()
    transform(0)
    table_copies[1].wait()
    leg_copy.start()
    transform(1)

    g2 = pltpu.make_async_remote_copy(
        src_ref=gat2.at[pl.ds(0, NWAVE - 1)], dst_ref=gat2.at[pl.ds(0, NWAVE - 1)], send_sem=s_g2s,
        recv_sem=s_g2r, device_id=(w, l), device_id_type=MESH,
    )
    g2.wait_send()
    g2.wait_recv()
    for r in range(4):
        total = gat2[8 * r]
        for i in range(1, 8):
            total = total + gat2[8 * r + i]
        gatv[r:r + 1, :] = jnp.clip(total, 0, PAIRS - 1)
    ids_copy = pltpu.make_async_copy(gatv, gats, s_local)
    ids_copy.start()
    ids_copy.wait()

    def packed(d):
        first = gats[d // 64, 2 * d % 128]
        second = gats[d // 64, 2 * d % 128 + 1]
        return jnp.concatenate([pairs[first], pairs[second]], axis=0).astype(BF16)

    recv_f[me] = packed(me)

    def send_forward(i, c):
        j = 256 - i
        w2 = wave_at(w, j % NWAVE)
        l2 = lev_at(l, j // NWAVE)
        d = w2 * NLEV + l2
        send_f[d] = packed(d)
        pltpu.make_async_remote_copy(
            src_ref=send_f.at[d], dst_ref=recv_f.at[me], send_sem=s_fs, recv_sem=s_fr.at[l],
            device_id=(w2, l2), device_id_type=MESH,
        ).start()
        return c

    lax.fori_loop(1, 256, send_forward, 0, unroll=5)

    leg_copy.wait()

    def relay(i, c):
        k = pl.multiple_of(i * 16, 16)
        for ch in range(8):
            x = raw[pl.ds(k, 16), ch].astype(F32)
            for s in range(2):
                leg[s, pl.ds(k, 16), ch * 128:(ch + 1) * 128] = x[:, s, :].astype(BF16)
        return c

    lax.fori_loop(0, 64, relay, 0, unroll=2)
    for ch in range(8):
        x = raw[1024, ch].astype(F32)
        for s in range(2):
            last[s, :, ch * 128:(ch + 1) * 128] = jnp.broadcast_to(x[s:s + 1], (16, 128)).astype(BF16)

    def field_of(g):
        core = (l + 1 + g // 16) % 2
        return (g // 4 % 4 * 2 + core) * 4 + g % 4

    def chosen(a, base, width):
        sub = sub_iota((8, width))
        k = base + lane_iota((8, width))
        is_a = k < WAVES - a
        parity = jnp.where(is_a, k % 2, (k + a) % 2)
        member = jnp.where(is_a, a % 2, 1 - a % 2)
        sel = (sub // 4 == parity) & (sub // 2 % 2 == member) & (k < ROWS)
        degree = jnp.where(is_a, a + k, k - 1)
        return sel, degree

    for s, a in enumerate((a0, a1)):
        sel, degree = chosen(a, 0, ROWP)
        level = degree.astype(F32)
        scaled = level * (level + 1.0) / (WAVES * (WAVES - 1.0))
        squared = scaled * scaled
        one = jnp.where(sel, 1.0, 0.0)

        def damp_body(f, c, s=s, squared=squared, one=one):
            row = pl.multiple_of(f * 8, 8)
            damp[s, pl.ds(row, 8), :] = one / (1.0 + diffusion[field_of(f)] * squared)
            return c

        lax.fori_loop(0, 32, damp_body, 0)

    def arrive(i, c):
        src = lev_from(l, 7 - i)

        def landed(count):
            pltpu.make_async_remote_copy(
                src_ref=send_f.at[pl.ds(0, count)], dst_ref=recv_f.at[pl.ds(0, count)],
                send_sem=s_fs, recv_sem=s_fr.at[src], device_id=(w, l), device_id_type=MESH,
            ).wait_recv()

        @pl.when(src == l)
        def _():
            landed(NWAVE - 1)

        @pl.when(src != l)
        def _():
            landed(NWAVE)

        for block in range(8):
            tiles = [recv_f[(4 * block + v) * NLEV + src].astype(F32) for v in range(4)]
            by_field = swap_lane(*tiles)
            for s in range(2):
                for pair in range(2):
                    row = pl.multiple_of(i // 4 * 128 + src // 2 * 32 + pair * 16, 16)
                    oper[s, pl.ds(row, 16), block * 128:(block + 1) * 128] = jnp.concatenate(
                        [
                            by_field[2 * pair][8 * s:8 * s + 8],
                            by_field[2 * pair + 1][8 * s:8 * s + 8],
                        ],
                        axis=0,
                    ).astype(BF16)
        return c

    def pick(half, s, a, x, start, width):
        sel, _ = chosen(a, start, width)
        lanes = pl.ds(start, width)
        for i in range(8):
            damped = []
            for g in (2 * i, 2 * i + 1):
                y = jnp.where(sel, x[8 * g:8 * g + 8], 0.0)
                y = y + pltpu.roll(y, 4, 0)
                y = y + pltpu.roll(y, 2, 0)
                f = field_of(16 * half + g)
                if width == 128:
                    spec[s, f, :, 1024:ROWS] = y[0:2, 0:1]
                else:
                    spec[s, f, :, lanes] = y[0:2]
                row = 128 * half + 8 * g
                damped.append(y * damp[s, row:row + 8, lanes])
            row = 128 * half + 16 * i
            dope[s, row:row + 16, lanes] = jnp.concatenate(damped, axis=0).astype(BF16)

    def legendre_step(half):
        mine = slice(128 * half, 128 * half + 128)

        def product(n, c):
            start = pl.multiple_of(n * 256, 256)
            for s, a in enumerate((a0, a1)):
                x = lax.dot_general(
                    oper[s, mine], leg[s, pl.ds(start, 256), :], NT, preferred_element_type=F32
                )
                pick(half, s, a, x, start, 256)
            return c

        lax.fori_loop(0, 4, product, 0, unroll=2)
        for s, a in enumerate((a0, a1)):
            rhs = jnp.concatenate([last[s]] * 8, axis=0)
            x = lax.dot_general(oper[s, mine], rhs, NT, preferred_element_type=F32)
            pick(half, s, a, x, 1024, 128)

        def inverse(n, c):
            start = pl.multiple_of(n * 256, 256)
            sign = jnp.where(sub_iota((1, 8, 256)) < 4, 1.0, -1.0)
            for s in range(2):
                x = lax.dot_general(
                    dope[s, mine, 0:1024], leg[s, 0:1024, pl.ds(start, 256)], NN,
                    preferred_element_type=F32,
                )
                edge = dope[s, mine, 1024:ROWP].astype(F32)[:, 0:1]
                x = x + edge * last[s, :, pl.ds(start, 256)].astype(F32)[0:1]
                x = x.reshape(16, 8, 256)
                modes[s, 16 * half:16 * half + 16, :, pl.ds(start, 256)] = (
                    x * sign + pltpu.roll(x, 4, 1)
                )
            return c

        lax.fori_loop(0, 4, inverse, 0, unroll=2)

    def send_group(i, c):
        l2 = lev_at(l, 7 - i)
        for block in range(8):
            lanes = slice(block * 128, (block + 1) * 128)
            tiles = [
                jnp.concatenate([modes[s, i // 4 * 16 + l2 // 2 * 4 + f, :, lanes] for s in range(2)], axis=0)
                for f in range(4)
            ]
            for u, x in enumerate(swap_lane(*tiles)):
                send_b[(4 * block + u) * NLEV + l2] = x.astype(BF16)

        def send_back(m, c):
            w2 = wave_at(w, 31 - m)
            d = w2 * NLEV + l2

            @pl.when(d != me)
            def _():
                pltpu.make_async_remote_copy(
                    src_ref=send_b.at[d], dst_ref=recv_b.at[me], send_sem=s_bs,
                    recv_sem=s_br.at[l], device_id=(w2, l2), device_id_type=MESH,
                ).start()

            return c

        lax.fori_loop(0, 32, send_back, 0, unroll=4)
        return c

    for half in range(2):
        lax.fori_loop(4 * half, 4 * half + 4, arrive, 0)
        legendre_step(half)
        lax.fori_loop(4 * half, 4 * half + 4, send_group, 0)
    recv_b[me] = send_b[me]

    holders = [jnp.zeros((1, 128), F32)] * 4
    for r in range(4):
        held = jnp.broadcast_to(gatv[r:r + 1, :].astype(F32), (128, 128)).T
        slot = (128 * r + sub_iota((128, 128))).astype(F32)
        for b in range(4):
            pair = (128 * b + lane_iota((128, 128))).astype(F32)
            hit = jnp.where(held == pair, slot, 0.0)
            holders[b] = holders[b] + jnp.sum(hit, axis=0, keepdims=True)
    holders = [holder.astype(jnp.int32) for holder in holders]

    for q in range(4):
        bases = [2 * lev_from(l, 7 - 2 * q - u) for u in range(2)]

        def onehot_body(b, c, q=q, bases=bases):
            sub = sub_iota((128, 128))
            slot = jnp.where(sub < 64, bases[0], bases[1]) + sub % 64 // 2 * 16 + sub % 2
            for b in range(4):
                hit = slot == holders[b]
                onehot[q * 128:(q + 1) * 128, b * 128:(b + 1) * 128] = jnp.where(
                    hit, 1.0, 0.0
                ).astype(BF16)
            return c

        lax.fori_loop(0, 1, onehot_body, 0)
    for h in range(2):
        column[h] = jnp.broadcast_to(band_points[h][0:1, :].astype(F32), (128, 128)).T

    def returned(q, c):
        for u in range(2):
            src = lev_from(l, 7 - 2 * q - u)

            def landed(count, src=src):
                pltpu.make_async_remote_copy(
                    src_ref=send_b.at[pl.ds(0, count)], dst_ref=recv_b.at[pl.ds(0, count)],
                    send_sem=s_bs, recv_sem=s_br.at[src], device_id=(w, l), device_id_type=MESH,
                ).wait_recv()

            @pl.when(src == l)
            def _():
                landed(NWAVE - 1)

            @pl.when(src != l)
            def _():
                landed(NWAVE)

            for v in range(NWAVE):
                both = recv_b[v * NLEV + src].astype(F32)
                rows[64 * u + 2 * v] = both[0:8]
                rows[64 * u + 2 * v + 1] = both[8:16]
        lanes = pl.multiple_of(q * 128, 128)
        for j in range(8):
            turned[j, :, pl.ds(lanes, 128)] = rows[:, j, :].T.astype(BF16)
        return c

    lax.fori_loop(0, 4, returned, 0)

    for h in range(2):
        for p in range(2):
            for r in range(2):
                x = lax.dot_general(
                    turned[4 * h + 2 * p + r], onehot[...], NN, preferred_element_type=F32
                )
                limit = jnp.concatenate([column[h]] * 4, axis=1)
                twice = twice_wave(p, lane_iota((128, PAIRS)))
                x = jnp.where(twice.astype(F32) < limit, x, 0.0)
                x = x * (jnp.where(twice == 0, 1.0, 2.0) if p == 0 else 2.0)
                back[p, h * 128:(h + 1) * 128, r * PAIRS:(r + 1) * PAIRS] = x.astype(BF16)

    def write(x, start, width):
        for h in range(2):
            for f in range(4):
                row = h * 128 + f * 32
                grid[f, h, :, start:start + width] = x[row:row + 32].astype(BF16)

    tail = None
    before = None
    for start, width in BLOCKS:
        x = jnp.dot(back[0], table[0, :, start:start + width], preferred_element_type=F32)
        y = jnp.dot(back[1], table[1, :, start:start + width], preferred_element_type=F32)
        total = x + y
        differ = pltpu.roll(x - y, 64, 1)
        if width == 128:
            tail = differ
            before = total
        else:
            low = lane_iota((256, 128)) < 64
            write(total, start, 256)
            edge = jnp.where(low, before, differ[:, :128])
            write(jnp.concatenate([edge, differ[:, 128:]], axis=1), 2048 + start, 256)
            before = differ[:, :128]
    write(jnp.where(lane_iota((256, 128)) < 64, before, tail), 4096, 128)

    pltpu.make_async_remote_copy(
        src_ref=send_f.at[pl.ds(0, 255)], dst_ref=recv_f.at[pl.ds(0, 255)], send_sem=s_fs,
        recv_sem=s_g1r, device_id=(w, l), device_id_type=MESH,
    ).wait_send()
    pltpu.make_async_remote_copy(
        src_ref=send_b.at[pl.ds(0, 255)], dst_ref=recv_b.at[pl.ds(0, 255)], send_sem=s_bs,
        recv_sem=s_g1r, device_id=(w, l), device_id_type=MESH,
    ).wait_send()


def shards(grid_field, legendre, wave_groups, lat_weights, cycle_points, diffusion):
    dma = pltpu.SemaphoreType.DMA
    vmem = pl.BlockSpec(memory_space=pltpu.VMEM)
    hbm = pl.BlockSpec(memory_space=pltpu.HBM)
    table = jnp.asarray(basis_tables())
    by_row = legendre.reshape(2, ROWS, 8, 128).transpose(1, 2, 0, 3)
    return pl.pallas_call(
        exchange,
        out_shape=(
            pltpu.VMEM((2, 32, 2, ROWS), F32),
            pltpu.VMEM((4, 2, 32, NLON), BF16),
        ),
        in_specs=[hbm] * 7,
        out_specs=(vmem, vmem),
        scratch_shapes=[
            pltpu.VMEM((4, 2, 32, NLON), BF16),
            pltpu.VMEM((ROWS, 8, 2, 128), BF16),
            pltpu.VMEM((2, 1024, 1024), BF16),
            pltpu.VMEM((2, 16, 1024), BF16),
            pltpu.VMEM((2, 1024, WIDE), BF16),
            pltpu.VMEM((2, 256, WIDE), BF16),
            pltpu.VMEM((PAIRS, 8, 128), F32),
            pltpu.VMEM((256, 16, 128), BF16),
            pltpu.VMEM((256, 16, 128), BF16),
            pltpu.VMEM((2, 256, 1024), BF16),
            pltpu.VMEM((2, 256, ROWP), F32),
            pltpu.VMEM((2, 256, ROWP), BF16),
            pltpu.VMEM((2, 32, 8, 1024), F32),
            pltpu.VMEM((256, 16, 128), BF16),
            pltpu.VMEM((256, 16, 128), BF16),
            pltpu.VMEM((128, 8, 128), F32),
            pltpu.VMEM((8, 128, PAIRS), BF16),
            pltpu.VMEM((PAIRS, PAIRS), BF16),
            pltpu.VMEM((2, 128, 128), F32),
            pltpu.VMEM((2, 256, 1024), BF16),
            pltpu.VMEM((NLEV, 1, 128), jnp.int32),
            pltpu.VMEM((NWAVE, 1, 128), jnp.int32),
            pltpu.VMEM((4, 128), jnp.int32),
            pltpu.SMEM((4, 128), jnp.int32),
            pltpu.SMEM((2,), jnp.int32),
            pltpu.VMEM((1, 1024), F32),
            pltpu.VMEM((2, 1024), jnp.int32),
            pltpu.SMEM((32,), F32),
            dma((2,)), dma, dma, dma, dma((4,)), dma, dma, dma, dma, dma, dma((NLEV,)), dma,
            dma((NLEV,)),
        ],
        compiler_params=pltpu.CompilerParams(
            collective_id=0, has_side_effects=True, vmem_limit_bytes=56 << 20
        ),
        name="exchange",
    )(grid_field, by_row, table, wave_groups, lat_weights.reshape(1, -1), cycle_points, diffusion)


def solution(mesh):
    return jax.shard_map(
        shards,
        mesh=mesh,
        in_specs=(
            P("lev", None, "wave", None),
            P(("wave", "lev"), None, None),
            P(("wave", "lev")),
            P(),
            P(),
            P(),
        ),
        out_specs=(P(("wave", "lev"), None, None, None), P("lev", None, "wave", None)),
        check_vma=False,
    )
```
